256 devices in a mesh: tm: 8 (over z), star: 32 (over x, y, core).
Axes of the slice: x: 4, y: 4, z: 8, core: 2. Of those that a mesh axis runs over, the one named last changes fastest.
Arguments:
- star_coef: float32 [5, 524288], P(None, ('tm', 'star')), may hold values from -6 to 6
- att_coef: float32 [12, 524288], P(None, ('tm', 'star')), may hold values from -6 to 6
- cal_coef: float32 [524288], P(('tm', 'star')), may hold values from -6 to 6
- observed: float32 [524288], P(('tm', 'star')), may hold values from -6 to 6
- star_index: int32 [524288], P(('tm', 'star')), may hold values from 0 to 4095
- knot_index: int32 [524288], P(('tm', 'star')), may hold values from 0 to 1023
- cal_index: int32 [524288], P(('tm', 'star')), may hold values from 0 to 2047
- valid_blocks: int32 [8, 32], P('tm', 'star'), may hold values from 6 to 16, as said below
Outputs:
- star_solution: float32 [5, 131072], P(None, 'star')
- attitude_solution: float32 [3, 8192], P(None, 'tm')
- calibration_solution: float32 [2048], replicated
The draws below stay inside these ranges and needn't reach their ends.
Inputs may be any that keep to these rules, and one draw needn't show every extreme that they name: `valid_blocks`: every value lies between the two bounds, and the largest is reached in every draw.
All inputs are finite; a program needn't handle non-finite values.
Results may differ from the reference program's by a relative error of at most 0.0003.
Values sent between devices are 32-bit elements; how exact they have to be, the bound alone decides.
No kernel may reach another device: no remote copies, remote signals or barrier semaphores. Data moves between devices by JAX's collectives and lax.ppermute only.
A program may use at most 64 MiB of HBM per device.

```python
import math
import jax
import jax.numpy as jnp
import numpy as np
from jax import lax

ROWS_DEV = 2048
STAR_DEV = 4096
KNOT_DEV = 1024
CAL = 2048
PAR = 5
ITERS = 3
STARS = 131072
KNOTS = 8192
ROWS = 524288
N_TM = 8
N_STAR = 32


def draw_valid_blocks(key, part):
    full = ROWS_DEV // 128
    lowest = (full + 2) // 3
    first_key, second_key = jax.random.split(key)
    blocks = jax.random.randint(first_key, (N_TM * N_STAR,), lowest, full + 1)
    chosen = jax.random.randint(second_key, (), 0, N_TM * N_STAR)
    blocks = jnp.where(jnp.arange(N_TM * N_STAR) == chosen, full, blocks)
    return blocks.reshape(N_TM, N_STAR).astype(jnp.int32)


def touch_ends(values, stream_key, low, largest):
    longest = values.shape.index(max(values.shape))
    spots = []
    for shift in (0, 1):
        where = [jax.random.randint(jax.random.fold_in(stream_key, axis), (), 0, length) for axis, length in enumerate(values.shape)]
        where[longest] = (where[longest] + shift) % values.shape[longest]
        spots.append(tuple(where))
    return values.at[spots[0]].set(low).at[spots[1]].set(largest)


def block_scale(own_key, dims, cuts, low, high):
    gain, own = 1.0, jax.random.fold_in(own_key, 6)
    for position, blocks in cuts:
        heights = jnp.exp(jax.random.uniform(jax.random.fold_in(own, position), (blocks,), jnp.float32, low / len(cuts), high / len(cuts)))
        gain = gain * jnp.repeat(heights, dims[position] // blocks).reshape([-1 if axis == position else 1 for axis in range(len(dims))])
    return gain


def rank_bounds(amount, slope):
    weights = [(1 << 20) // math.isqrt(rank ** slope) + 1 for rank in range(1, amount + 1)]
    scale = 1 + sum(weights) // (1 << 30)
    return np.cumsum(np.array([max(1, weight // scale) for weight in weights]))


def skewed_ids(stream_key, shape, amount, skew):
    listing = rank_bounds(amount, skew)
    ticket = jax.random.randint(jax.random.fold_in(stream_key, 1), shape, 0, int(listing[amount - 1]))
    rank = jnp.searchsorted(jnp.asarray(listing, jnp.int32), ticket, side="right")
    return jax.random.permutation(jax.random.fold_in(stream_key, 2), amount)[rank].astype(jnp.int32)


def bell_draw(stream_key, shape, scale, reach, cuts=(), held_as=jnp.bfloat16):
    entries = jax.random.normal(stream_key, shape, jnp.float32) * scale
    if len(cuts) > 0:
        entries = block_scale(stream_key, shape, cuts, -0.22, 0.18) * entries
    return jnp.clip(entries, min=-reach, max=reach).astype(held_as)


def setup_inputs(seed: int = 0) -> dict:
    key_of = jax.random.split(jax.random.key(seed), 9)
    return {
        "star_coef": bell_draw(key_of[0], (PAR, ROWS), 1.0, 6.0, ((1, 256),), jnp.float32),
        "att_coef": bell_draw(key_of[1], (12, ROWS), 0.5, 6.0, ((1, 256),), jnp.float32),
        "cal_coef": bell_draw(key_of[2], (ROWS,), 1.0, 6.0, ((0, 256),), jnp.float32),
        "observed": bell_draw(key_of[3], (ROWS,), 1.0, 6.0, ((0, 256),), jnp.float32),
        "star_index": touch_ends(skewed_ids(key_of[4], (ROWS,), STAR_DEV, 2), jax.random.fold_in(key_of[4], 3), 0, STAR_DEV - 1).astype(jnp.int32),
        "knot_index": touch_ends(jax.random.randint(key_of[5], (ROWS,), 0, KNOT_DEV), jax.random.fold_in(key_of[5], 1), 0, KNOT_DEV - 1).astype(jnp.int32),
        "cal_index": touch_ends(jax.random.randint(key_of[6], (ROWS,), 0, CAL), jax.random.fold_in(key_of[6], 1), 0, CAL - 1).astype(jnp.int32),
        "valid_blocks": draw_valid_blocks(jax.random.fold_in(key_of[8], 71), 0),
    }


def reference(star_coef, att_coef, cal_coef, observed, star_index, knot_index, cal_index, valid_blocks):
    places = jnp.arange(ROWS, dtype=jnp.int32)
    device = places // ROWS_DEV
    tpos = device // N_STAR
    spos = device % N_STAR
    local = places % ROWS_DEV
    live = (local < 128 * valid_blocks.reshape(-1)[device]).astype(jnp.float32)
    star_glob = spos * STAR_DEV + star_index
    knot_glob = tpos * KNOT_DEV + knot_index

    def forward(parts):
        stars, knots, cals = parts
        padded = jnp.pad(knots, ((0, 0), (0, 3)))
        total = lax.optimization_barrier(jnp.sum(star_coef * jnp.take(stars, star_glob, axis=1), axis=0))
        for j in range(4):
            taken = jnp.take(padded, knot_glob + j, axis=1)
            total = total + lax.optimization_barrier(jnp.sum(att_coef[3 * j:3 * j + 3] * taken, axis=0))
        total = total + cal_coef * cals[cal_index]
        return total * live

    def adjoint(rows_vec):
        masked = rows_vec * live
        stars = jnp.stack([jax.ops.segment_sum(star_coef[p] * masked, star_glob, num_segments=STARS) for p in range(PAR)])
        knots = []
        for a in range(3):
            values = jnp.concatenate([att_coef[3 * j + a] * masked for j in range(4)])
            where = jnp.concatenate([knot_glob + j for j in range(4)])
            knots.append(jax.ops.segment_sum(values, where, num_segments=KNOTS + 3)[:KNOTS])
        knots = jnp.stack(knots)
        cals = jax.ops.segment_sum(cal_coef * masked, cal_index, num_segments=CAL)
        return (stars, knots, cals)

    def square(parts):
        return sum((jnp.sum(item * item) for item in parts))
    rhs = observed * live
    vec = (jnp.zeros((PAR, STARS), jnp.float32), jnp.zeros((3, KNOTS), jnp.float32), jnp.zeros((CAL,), jnp.float32))
    alpha = jnp.float32(0.0)
    rowvec = rhs
    for step in range(ITERS + 1):
        if step == 0:
            upd = rhs
        else:
            upd = forward(vec) - alpha * rowvec
        beta = jnp.sqrt(jnp.sum(upd * upd))
        rowvec = upd / beta
        image = adjoint(rowvec)
        nextv = tuple((qi - beta * vi for qi, vi in zip(image, vec)))
        alpha = jnp.sqrt(square(nextv))
        vec = tuple((item / alpha for item in nextv))
        if step == 0:
            sol = tuple((jnp.zeros_like(item) for item in vec))
            wdir = vec
            phibar = beta
            rhobar = alpha
        else:
            rho = jnp.sqrt(rhobar * rhobar + beta * beta)
            cosv = rhobar / rho
            sinv = beta / rho
            theta = sinv * alpha
            rhobar = -cosv * alpha
            phi = cosv * phibar
            phibar = sinv * phibar
            sol = tuple((xi + phi / rho * wi for xi, wi in zip(sol, wdir)))
            wdir = tuple((vi - theta / rho * wi for vi, wi in zip(vec, wdir)))
    return (sol[0], sol[1], sol[2])
```

```python
import functools

import jax
import jax.numpy as jnp
from jax import lax
from jax.experimental import pallas as pl
from jax.experimental.pallas import tpu as pltpu
from jax.sharding import PartitionSpec as P

ROWS = 2048
LO = 128
CHUNK = 512
N_S, N_C, N_B, N_K = 160, 16, 8, 24
N_ALL = N_S + N_C + N_B + N_K
N_Z = N_S + N_C + N_B
SCALAR_LANE = 64
F32, BF16 = jnp.float32, jnp.bfloat16


def iota(shape, axis):
    return lax.broadcasted_iota(jnp.int32, shape, axis)


def split(value):
    first = value.astype(BF16)
    return first, (value - first.astype(F32)).astype(BF16)


def total(value):
    return jnp.sum(jnp.sum(value, axis=1, keepdims=True), axis=0, keepdims=True)


def one_hot(index, count):
    return jnp.where(iota((count, index.shape[1]), 0) == index, 1.0, 0.0)


def chunk_hots(index_ref, columns, count):
    index = index_ref[:, columns]
    low = one_hot(index & (LO - 1), LO).astype(BF16)
    return low, one_hot(index >> 7, count)


def left_shift(knots, following, j):
    if j == 0:
        return knots
    rolled = pltpu.roll(knots, LO - j, 1)
    upper = pltpu.roll(rolled, 7, 0)
    ahead = pltpu.roll(jnp.broadcast_to(following, (8, LO)), LO - j, 1)
    upper = jnp.where(iota((8, LO), 0) == 7, ahead, upper)
    return jnp.where(iota((8, LO), 1) < LO - j, rolled, upper)


def head_rows(bounds, window):
    row = jnp.sum(jnp.where(iota((8, LO), 0) == window, bounds, 0.0), axis=0, keepdims=True)
    lane = iota((1, LO), 1)
    return [jnp.where(lane < 3, row if a == 0 else pltpu.roll(row, LO - 8 * a, 1), 0.0) for a in range(3)]


def with_heads(vec, window):
    bounds = vec[N_S + N_C : N_Z]
    own, following = head_rows(bounds, window), head_rows(bounds, window + 1)
    knots = []
    for a in range(3):
        part = vec[N_Z + 8 * a : N_Z + 8 * a + 8]
        knots.append(part + jnp.where(iota((8, LO), 0) == 0, jnp.broadcast_to(own[a], (8, LO)), 0.0))
    return knots, following


def forward(vec, window, refs, live, out_ref):
    star_ref, att_ref, cal_ref, _, si_ref, ki_ref, ci_ref = refs
    knots, following = with_heads(vec, window)
    shifted = jnp.concatenate(
        [left_shift(knots[a], following[a], j) for j in range(4) for a in range(3)], axis=0
    )
    tables = [
        jnp.concatenate(split(table), axis=1)
        for table in (vec[:N_S], shifted, vec[N_S : N_S + N_C])
    ]
    for start in range(0, ROWS, CHUNK):
        columns = pl.ds(start, CHUNK)
        result = None
        for table, index_ref, coef_ref, count in zip(
            tables, (si_ref, ki_ref, ci_ref), (star_ref, att_ref, cal_ref), (32, 8, 16)
        ):
            low, high = chunk_hots(index_ref, columns, count)
            taken = jnp.dot(table, jnp.concatenate([low, low], axis=0), preferred_element_type=F32)
            mixed = None
            for p in range(coef_ref.shape[0]):
                term = coef_ref[p : p + 1, columns] * taken[p * count : (p + 1) * count]
                mixed = term if mixed is None else mixed + term
            mixed = mixed * high
            for part in range(0, count, 8):
                piece = mixed[part : part + 8]
                result = piece if result is None else result + piece
        out_ref[:, columns] = jnp.sum(result, axis=0, keepdims=True) * live[:, start : start + CHUNK]


def adjoint(row_ref, window, refs):
    star_ref, att_ref, cal_ref, _, si_ref, ki_ref, ci_ref = refs
    sums = [None, None, None]
    for start in range(0, ROWS, CHUNK):
        columns = pl.ds(start, CHUNK)
        row = row_ref[:, columns]
        for which, (index_ref, coef_ref, count) in enumerate(
            zip((si_ref, ki_ref, ci_ref), (star_ref, att_ref, cal_ref), (32, 8, 16))
        ):
            low, high = chunk_hots(index_ref, columns, count)
            pieces = split(coef_ref[:, columns] * row)
            left = jnp.concatenate(
                [
                    (high * piece[p : p + 1].astype(F32)).astype(BF16)
                    for piece in pieces
                    for p in range(coef_ref.shape[0])
                ],
                axis=0,
            )
            added = lax.dot_general(left, low, (((1,), (1,)), ((), ())), preferred_element_type=F32)
            sums[which] = added if sums[which] is None else sums[which] + added
    stars, spread, cals = (item[: item.shape[0] // 2] + item[item.shape[0] // 2 :] for item in sums)
    rows, lanes = iota((8, LO), 0), iota((8, LO), 1)
    knots, heads, tails = [], 0.0, 0.0
    for a in range(3):
        own, over = spread[8 * a : 8 * a + 8], jnp.zeros((8, LO), F32)
        for j in range(1, 4):
            rolled = pltpu.roll(spread[24 * j + 8 * a : 24 * j + 8 * a + 8], j, 1)
            wrapped = pltpu.roll(rolled, 1, 0)
            own = own + jnp.where(lanes >= j, rolled, jnp.where(rows > 0, wrapped, 0.0))
            over = over + jnp.where(lanes < j, wrapped, 0.0)
        is_head = jnp.logical_and(rows == 0, lanes < 3)
        knots.append(jnp.where(is_head, 0.0, own))
        head, tail = jnp.where(is_head, own, 0.0), jnp.where(rows == 0, over, 0.0)
        if a > 0:
            head, tail = pltpu.roll(head, 8 * a, 1), pltpu.roll(tail, 8 * a, 1)
        heads, tails = heads + head, tails + tail
    head = jnp.broadcast_to(heads[:1], (8, LO))
    tail = jnp.broadcast_to(tails[:1], (8, LO))
    bounds = jnp.where(rows == window, head, 0.0) + jnp.where(rows == window + 1, tail, 0.0)
    return stars, cals, bounds, jnp.concatenate(knots, axis=0)


def write_sums(parts, scalars, scale, sum_refs):
    stars, cals, bounds, knots = parts
    wide_ref, knot_ref = sum_refs
    rows, lanes = iota((8, LO), 0), iota((8, LO), 1)
    block = bounds * scale
    for i, scalar in enumerate(scalars):
        block = jnp.where(jnp.logical_and(rows == i, lanes == SCALAR_LANE), jnp.broadcast_to(scalar, (8, LO)), block)
    wide_ref[:N_S] = stars * scale
    wide_ref[N_S : N_S + N_C] = cals * scale
    wide_ref[N_S + N_C :] = block
    knot_ref[...] = knots * scale


def read_sums(stars_ref, rest_ref):
    rest = rest_ref[...]
    bounds = rest[N_C : N_C + N_B]
    rows, lanes = iota((8, LO), 0), iota((8, LO), 1)
    scalars = [
        total(jnp.where(jnp.logical_and(rows == i, lanes == SCALAR_LANE), bounds, 0.0)) for i in range(3)
    ]
    bounds = jnp.where(lanes < SCALAR_LANE, bounds, 0.0)
    vec = jnp.concatenate([stars_ref[...], rest[:N_C], bounds, rest[N_C + N_B :]], axis=0)
    return vec, scalars


def square(vec):
    part = vec * vec
    return (
        total(part[:N_S]) * (1.0 / 8)
        + total(part[N_S:N_Z]) * (1.0 / 256)
        + total(part[N_Z:]) * (1.0 / 32)
    )


def live_rows(blocks_ref):
    return jnp.where(iota((1, ROWS), 1) < 128 * blocks_ref[0, 0], 1.0, 0.0)


def keep(scalars, ref):
    rows = iota((8, LO), 0)
    block = jnp.zeros((8, LO), F32)
    for i, scalar in enumerate(scalars):
        block = jnp.where(rows == i, jnp.broadcast_to(scalar, (8, LO)), block)
    ref[...] = block


def kept(ref):
    return [ref[i : i + 1, 0:1] for i in range(8)]


def start_kernel(blocks_ref, window_ref, *args):
    refs, (wide_ref, knot_ref, row_ref) = args[:7], args[7:]
    live = live_rows(blocks_ref)
    row_ref[...] = refs[3][...] * live
    norm = total(row_ref[...] * row_ref[...])
    size = 0.0
    for coef_ref in refs[:3]:
        coef = coef_ref[...]
        size = size + total(jnp.sum(coef * coef, axis=0, keepdims=True) * live)
    write_sums(adjoint(row_ref, window_ref[0], refs), [norm, size], 1.0, (wide_ref, knot_ref))


def first_kernel(blocks_ref, window_ref, *args):
    refs, (stars_ref, rest_ref), outs = args[:7], args[7:9], args[9:]
    wide_ref, knot_ref, grad_ref, row_ref, kept_ref = outs
    live = live_rows(blocks_ref)
    vec, (norm, size, _) = read_sums(stars_ref, rest_ref)
    inverse, length = lax.rsqrt(size), jnp.sqrt(norm)
    grad = vec * inverse / length
    grad_ref[...] = grad
    forward(grad, window_ref[0], refs, live * inverse, row_ref)
    row = row_ref[...]
    keep([inverse, length], kept_ref)
    parts = adjoint(row_ref, window_ref[0], refs)
    write_sums(parts, [square(grad), total(row * row)], inverse, (wide_ref, knot_ref))


def second_kernel(blocks_ref, window_ref, *args):
    refs, (stars_ref, rest_ref, grad_ref, q_ref, old_ref), outs = args[:7], args[7:12], args[12:]
    wide_ref, knot_ref, new_ref, image_ref, row_ref, kept_ref = outs
    live = live_rows(blocks_ref)
    inverse, length = kept(old_ref)[:2]
    image, (gamma, delta, _) = read_sums(stars_ref, rest_ref)
    image_ref[...] = image
    grad = grad_ref[...] - (gamma / delta) * image
    new_ref[...] = grad
    forward(grad, window_ref[0], refs, live * inverse, row_ref)
    row = row_ref[...]
    keep([inverse, length, gamma, delta], kept_ref)
    parts = adjoint(row_ref, window_ref[0], refs)
    write_sums(parts, [square(grad), total(row * row), total(row * q_ref[...])], inverse, (wide_ref, knot_ref))


def third_kernel(blocks_ref, window_ref, *args):
    refs, ins, outs = args[:7], args[7:15], args[15:]
    stars_ref, rest_ref, first_ref, grad_ref, image_ref, q_ref, row_ref, old_ref = ins
    new_ref, x_ref, direction_ref, kept_ref, scalar_ref, work_ref = outs
    live = live_rows(blocks_ref)
    inverse, length, gamma0, delta0 = kept(old_ref)[:4]
    image, (gamma1, square1, cross1) = read_sums(stars_ref, rest_ref)
    beta = gamma1 / gamma0
    first, grad = first_ref[...], grad_ref[...]
    direction = grad + beta * first
    q = row_ref[...] + beta * q_ref[...]
    delta1 = square1 + 2.0 * beta * cross1 + beta * beta * delta0
    image = image + beta * image_ref[...]
    step = gamma1 / delta1
    x_ref[...] = (gamma0 / delta0) * first + step * direction
    direction_ref[...] = direction
    grad = grad - step * image
    new_ref[...] = grad
    forward(grad, window_ref[0], refs, live * inverse, work_ref)
    row = work_ref[...]
    keep([inverse, length, gamma1, delta1], kept_ref)
    lane = iota((1, LO), 1)
    scalar_ref[...] = (
        jnp.where(lane == 0, square(grad), 0.0)
        + jnp.where(lane == 1, total(row * row), 0.0)
        + jnp.where(lane == 2, total(row * q), 0.0)
    )


def last_kernel(window_ref, sums_ref, grad_ref, x_ref, direction_ref, old_ref, star_ref, att_ref, cal_ref):
    inverse, length, gamma1, delta1 = kept(old_ref)[:4]
    sums = jnp.sum(sums_ref[...], axis=0, keepdims=True)
    gamma2, square2, cross2 = (sums[:, i : i + 1] for i in range(3))
    beta = gamma2 / gamma1
    delta2 = square2 + 2.0 * beta * cross2 + beta * beta * delta1
    direction = grad_ref[...] + beta * direction_ref[...]
    x = (x_ref[...] + (gamma2 / delta2) * direction) * (inverse * length)
    for hi in range(32):
        for p in range(5):
            star_ref[p : p + 1, LO * hi : LO * hi + LO] = x[32 * p + hi : 32 * p + hi + 1]
    knots, _ = with_heads(x, window_ref[0])
    for a in range(3):
        for hi in range(8):
            att_ref[a : a + 1, LO * hi : LO * hi + LO] = knots[a][hi : hi + 1]
    cal_ref[...] = x[N_S : N_S + N_C]


def call(kernel, smem, vmem, outs, scratch=()):
    return pl.pallas_call(
        kernel,
        out_shape=[jax.ShapeDtypeStruct(shape, F32) for shape in outs],
        in_specs=[pl.BlockSpec(memory_space=pltpu.SMEM)] * len(smem)
        + [pl.BlockSpec(memory_space=pltpu.VMEM)] * len(vmem),
        out_specs=[pl.BlockSpec(memory_space=pltpu.VMEM)] * len(outs),
        scratch_shapes=list(scratch),
        compiler_params=pltpu.CompilerParams(vmem_limit_bytes=40 * 1024 * 1024),
    )(*smem, *vmem)


def swap(value, axis, bits):
    count = lax.axis_size(axis)
    return lax.ppermute(value, axis, [(i, i ^ bits) for i in range(count)])


def reduce(wide, knots):
    for bits in (1, 2, 6):
        wide = wide + swap(wide, "tm", bits)
    rest = jnp.concatenate([wide[N_S:], knots], axis=0)
    rest = rest + swap(rest, "star", 1)
    for near, wrap, far in ((8, 24, 16), (2, 6, 4)):
        arrived = [swap(rest, "star", bits) for bits in (near, wrap, far)]
        rest = (rest + arrived[0]) + (arrived[1] + arrived[2])
    return wide[:N_S], rest


def shards(star_coef, att_coef, cal_coef, observed, star_index, knot_index, cal_index, valid_blocks):
    window = lax.axis_index("tm").astype(jnp.int32).reshape(1)
    smem = (valid_blocks, window)
    rows = (
        star_coef,
        att_coef,
        cal_coef.reshape(1, ROWS),
        observed.reshape(1, ROWS),
        star_index.reshape(1, ROWS),
        knot_index.reshape(1, ROWS),
        cal_index.reshape(1, ROWS),
    )
    wide_shape, knot_shape, vec_shape = (N_Z, LO), (N_K, LO), (N_ALL, LO)
    row_shape, small = (1, ROWS), (8, LO)
    sums = (wide_shape, knot_shape)
    row_scratch = [pltpu.VMEM(row_shape, F32)]
    wide, knots = call(start_kernel, smem, rows, sums, row_scratch)
    arrived = reduce(wide, knots)
    wide, knots, grad0, row0, scalars = call(
        first_kernel, smem, rows + arrived, sums + (vec_shape, row_shape, small)
    )
    arrived = reduce(wide, knots)
    wide, knots, grad1, image0, row1, scalars = call(
        second_kernel,
        smem,
        rows + arrived + (grad0, row0, scalars),
        sums + (vec_shape, vec_shape, row_shape, small),
    )
    arrived = reduce(wide, knots)
    grad2, x, direction, scalars, partial = call(
        third_kernel,
        smem,
        rows + arrived + (grad0, grad1, image0, row0, row1, scalars),
        (vec_shape, vec_shape, vec_shape, small, (1, LO)),
        row_scratch,
    )
    count = lax.axis_size("tm") * lax.axis_size("star")
    everyone = lax.all_to_all(
        jnp.broadcast_to(partial[None], (count, 1, LO)), ("tm", "star"), 0, 0
    ).reshape(count, LO)
    stars, attitude, cals = call(
        last_kernel,
        (window,),
        (everyone, grad2, x, direction, scalars),
        ((5, 4096), (3, 1024), (N_C, LO)),
    )
    return stars, attitude, cals.reshape(-1)


def solution(mesh):
    by_row = P(("tm", "star"))
    return jax.shard_map(
        shards,
        mesh=mesh,
        in_specs=(P(None, ("tm", "star")), P(None, ("tm", "star"))) + (by_row,) * 5 + (P("tm", "star"),),
        out_specs=(P(None, "star"), P(None, "tm"), P()),
        check_vma=False,
    )
```

```python
import jax
import jax.numpy as jnp
from jax import lax
from jax.experimental import pallas as pl
from jax.experimental.pallas import tpu as pltpu
from jax.sharding import Mesh
from jax.sharding import PartitionSpec as P

ROWS = 2048
LO = 128
MASKS = (0, 2, 4, 6)
REST = (1,)
GROUP = len(MASKS)
BITS = 0
for _mask in MASKS:
    BITS |= _mask
N_S, N_C, N_B, N_K = 160, 16, 8, 24
N_Z = N_S + N_C + N_B
N_ALL = N_Z + N_K * GROUP
STAR, ATT, CAL, INDEX, RIGHT, PACKED = 0, 5, 17, 18, 21, 24
PARTS = ((STAR, 5, 32), (ATT, 12, 8), (CAL, 1, 16))
SCALAR_LANE = 64
TM = ("tm_high", "tm_low")
F32, BF16 = jnp.float32, jnp.bfloat16


def iota(shape, axis):
    return lax.broadcasted_iota(jnp.int32, shape, axis)


def member_of(window):
    return (window >> 1) & (GROUP - 1)


def window_of(window, member):
    return (window & ~BITS) | (member << 1)


def split(value):
    first = value.astype(BF16)
    return first, (value - first.astype(F32)).astype(BF16)


def total(value):
    return jnp.sum(jnp.sum(value, axis=1, keepdims=True), axis=0, keepdims=True)


def one_hot(index, count):
    return jnp.where(iota((count, index.shape[1]), 0) == index, 1.0, 0.0)


def left_shift(knots, following, j):
    if j == 0:
        return knots
    rolled = pltpu.roll(knots, LO - j, 1)
    upper = pltpu.roll(rolled, 7, 0)
    ahead = pltpu.roll(jnp.broadcast_to(following, (8, LO)), LO - j, 1)
    upper = jnp.where(iota((8, LO), 0) == 7, ahead, upper)
    return jnp.where(iota((8, LO), 1) < LO - j, rolled, upper)


def head_rows(bounds, window):
    row = jnp.sum(jnp.where(iota((8, LO), 0) == window, bounds, 0.0), axis=0, keepdims=True)
    lane = iota((1, LO), 1)
    return [
        jnp.where(lane < 3, row if a == 0 else pltpu.roll(row, LO - 8 * a, 1), 0.0) for a in range(3)
    ]


def with_heads(vec_ref, window, member):
    bounds = vec_ref[N_S + N_C : N_Z]
    own, following = head_rows(bounds, window), head_rows(bounds, window + 1)
    knots = []
    for a in range(3):
        part = vec_ref[pl.ds(pl.multiple_of(N_Z + N_K * member + 8 * a, 8), 8)]
        knots.append(part + jnp.where(iota((8, LO), 0) == 0, jnp.broadcast_to(own[a], (8, LO)), 0.0))
    return knots, following


def shifted_knots(vec_ref, window, member):
    knots, following = with_heads(vec_ref, window, member)
    return jnp.concatenate(
        [left_shift(knots[a], following[a], j) for j in range(4) for a in range(3)], axis=0
    )


def hots_of(data_ref, slot, kinds):
    places = iota((LO, ROWS), 0).astype(F32).astype(BF16)
    hots = []
    for kind in kinds:
        index = data_ref[slot, INDEX + kind : INDEX + kind + 1].astype(jnp.int32)
        low = (index & (LO - 1)).astype(F32).astype(BF16)
        low = jnp.where(places == low, jnp.ones((), BF16), jnp.zeros((), BF16))
        hots.append((PARTS[kind], low, one_hot(index >> 7, PARTS[kind][2])))
    return hots


def forward(data_ref, slot, hots, tables):
    result = None
    for ((base, coefs, count), low, high), table in zip(hots, tables):
        taken = jnp.dot(table, jnp.concatenate([low, low], axis=0), preferred_element_type=F32)
        mixed = None
        for p in range(coefs):
            term = data_ref[slot, base + p : base + p + 1] * taken[p * count : (p + 1) * count]
            mixed = term if mixed is None else mixed + term
        mixed = mixed * high
        for part in range(0, count, 8):
            piece = mixed[part : part + 8]
            result = piece if result is None else result + piece
    return jnp.sum(result, axis=0, keepdims=True)


def adjoint(data_ref, slot, hots, row):
    sums = []
    for (base, coefs, count), low, high in hots:
        pieces = split(data_ref[slot, base : base + coefs] * row)
        left = jnp.concatenate(
            [
                (high * piece[p : p + 1].astype(F32)).astype(BF16)
                for piece in pieces
                for p in range(coefs)
            ],
            axis=0,
        )
        sums.append(lax.dot_general(left, low, (((1,), (1,)), ((), ())), preferred_element_type=F32))
    return sums


def fold(sums):
    return sums[: sums.shape[0] // 2] + sums[sums.shape[0] // 2 :]


def knot_sums(spread, window):
    rows, lanes = iota((8, LO), 0), iota((8, LO), 1)
    knots, heads, tails = [], 0.0, 0.0
    for a in range(3):
        own, over = spread[8 * a : 8 * a + 8], jnp.zeros((8, LO), F32)
        for j in range(1, 4):
            rolled = pltpu.roll(spread[24 * j + 8 * a : 24 * j + 8 * a + 8], j, 1)
            wrapped = pltpu.roll(rolled, 1, 0)
            own = own + jnp.where(lanes >= j, rolled, jnp.where(rows > 0, wrapped, 0.0))
            over = over + jnp.where(lanes < j, wrapped, 0.0)
        is_head = jnp.logical_and(rows == 0, lanes < 3)
        knots.append(jnp.where(is_head, 0.0, own))
        head, tail = jnp.where(is_head, own, 0.0), jnp.where(rows == 0, over, 0.0)
        if a > 0:
            head, tail = pltpu.roll(head, 8 * a, 1), pltpu.roll(tail, 8 * a, 1)
        heads, tails = heads + head, tails + tail
    head = jnp.broadcast_to(heads[:1], (8, LO))
    tail = jnp.broadcast_to(tails[:1], (8, LO))
    bounds = jnp.where(rows == window, head, 0.0) + jnp.where(rows == window + 1, tail, 0.0)
    return jnp.concatenate(knots, axis=0), bounds


def set_scalars(ref, base, scalars):
    rows, lanes = iota((8, LO), 0), iota((8, LO), 1)
    block = ref[base:]
    for i, scalar in enumerate(scalars):
        here = jnp.logical_and(rows == i, lanes == SCALAR_LANE)
        block = jnp.where(here, jnp.broadcast_to(scalar, (8, LO)), block)
    ref[base:] = block


def get_scalars(rest_ref):
    bounds = rest_ref[N_C : N_C + N_B]
    rows, lanes = iota((8, LO), 0), iota((8, LO), 1)
    return [
        total(jnp.where(jnp.logical_and(rows == i, lanes == SCALAR_LANE), bounds, 0.0)) for i in range(3)
    ]


def read_sums(stars_ref, rest_ref):
    bounds = jnp.where(iota((8, LO), 1) < SCALAR_LANE, rest_ref[N_C : N_C + N_B], 0.0)
    return jnp.concatenate([stars_ref[...], rest_ref[:N_C], bounds, rest_ref[N_C + N_B :]], axis=0)


def square(vec):
    part = vec * vec
    return (
        total(part[:N_S]) * (GROUP / 8)
        + total(part[N_S:N_Z]) * (GROUP / 256)
        + total(part[N_Z:]) * (1 / 32)
    )


def keep(scalars, ref):
    rows = iota((8, LO), 0)
    block = jnp.zeros((8, LO), F32)
    for i, scalar in enumerate(scalars):
        block = jnp.where(rows == i, jnp.broadcast_to(scalar, (8, LO)), block)
    ref[...] = block


def kept(ref):
    return [ref[i : i + 1, 0:1] for i in range(8)]


def start_kernel(blocks_ref, *args):
    sources, data_ref, scratch = args[:7], args[7], args[8:]
    held, semaphore = scratch[:7], scratch[7]
    copies = [
        pltpu.make_async_copy(source, target, semaphore.at[i])
        for i, (source, target) in enumerate(zip(sources, held))
    ]
    for copy in copies:
        copy.start()
    for copy in copies:
        copy.wait()
    live = jnp.where(iota((1, ROWS), 1) < 128 * blocks_ref[0, 0], 1.0, 0.0)
    data_ref[0, STAR : STAR + 5] = held[0][...] * live
    data_ref[0, ATT : ATT + 12] = held[1][...] * live
    data_ref[0, CAL : CAL + 1] = held[2][...] * live
    for which in range(3):
        data_ref[0, INDEX + which : INDEX + which + 1] = held[4 + which][...].astype(F32)
    data_ref[0, RIGHT : RIGHT + 1] = held[3][...] * live
    data_ref[0, RIGHT + 1 :] = jnp.zeros((PACKED - RIGHT - 1, ROWS), F32)


def gather_kernel(window_ref, data_ref, *args):
    wide_ref, knot_ref, star_ref, cal_ref = args
    window = window_ref[0]
    clear((wide_ref, star_ref, cal_ref))
    norm, size = 0.0, 0.0
    for member in range(GROUP):
        slot = member_of(window) ^ member
        row = data_ref[slot, RIGHT : RIGHT + 1]
        coefs = data_ref[slot, :INDEX]
        norm += total(row * row)
        size += total(jnp.sum(coefs * coefs, axis=0, keepdims=True))
        hots = hots_of(data_ref, slot, (0, 1, 2))
        add_sums(data_ref, slot, hots, row, window, member, args)
    finish_sums(args)
    set_scalars(wide_ref, N_S + N_C, [norm, size])


def clear(refs):
    for ref in refs:
        ref[...] = jnp.zeros(ref.shape, F32)


def add_sums(data_ref, slot, hots, row, window, member, sums):
    wide_ref, knot_ref, star_ref, cal_ref = sums
    stars, spread, cals = adjoint(data_ref, slot, hots, row)
    star_ref[...] += stars
    cal_ref[...] += cals
    knots, bounds = knot_sums(fold(spread), window_of(window, member))
    knot_ref[N_K * member : N_K * member + N_K] = knots
    wide_ref[N_S + N_C :] += bounds


def finish_sums(sums):
    wide_ref, _, star_ref, cal_ref = sums
    wide_ref[:N_S] = fold(star_ref[...])
    wide_ref[N_S : N_S + N_C] = fold(cal_ref[...])


def apply(window, vec_ref, data_ref, scale, row_ref, sums=None):
    vec = vec_ref[:N_Z]
    star_table = jnp.concatenate(split(vec[:N_S]), axis=1)
    cal_table = jnp.concatenate(split(vec[N_S : N_S + N_C]), axis=1)
    if sums is not None:
        clear((sums[0], sums[2], sums[3]))
    for member in range(GROUP):
        slot = member_of(window) ^ member
        knots = shifted_knots(vec_ref, window_of(window, member), member)
        tables = (star_table, jnp.concatenate(split(knots), axis=1), cal_table)
        hots = hots_of(data_ref, slot, (0, 1, 2))
        row = forward(data_ref, slot, hots, tables) * scale
        row_ref[member : member + 1] = row
        if sums is not None:
            add_sums(data_ref, slot, hots, row * scale, window, member, sums)
    if sums is not None:
        finish_sums(sums)


def first_kernel(window_ref, data_ref, stars_ref, rest_ref, *args):
    wide_ref, knot_ref, grad_ref, row_ref, kept_ref, star_ref, cal_ref = args
    window = window_ref[0]
    norm, size, _ = get_scalars(rest_ref)
    inverse, length = lax.rsqrt(size), jnp.sqrt(norm)
    grad = read_sums(stars_ref, rest_ref) * inverse / length
    grad_ref[...] = grad
    keep([inverse, length], kept_ref)
    apply(window, grad_ref, data_ref, inverse, row_ref, (wide_ref, knot_ref, star_ref, cal_ref))
    row = row_ref[...]
    set_scalars(wide_ref, N_S + N_C, [square(grad), total(row * row)])


def second_kernel(window_ref, data_ref, stars_ref, rest_ref, grad_ref, q_ref, old_ref, *args):
    wide_ref, knot_ref, new_ref, image_ref, row_ref, kept_ref, star_ref, cal_ref = args
    inverse, length = kept(old_ref)[:2]
    gamma, delta, _ = get_scalars(rest_ref)
    image = read_sums(stars_ref, rest_ref)
    image_ref[...] = image
    grad = grad_ref[...] - (gamma / delta) * image
    new_ref[...] = grad
    keep([inverse, length, gamma, delta], kept_ref)
    sums = (wide_ref, knot_ref, star_ref, cal_ref)
    apply(window_ref[0], new_ref, data_ref, inverse, row_ref, sums)
    row = row_ref[...]
    set_scalars(wide_ref, N_S + N_C, [square(grad), total(row * row), total(row * q_ref[...])])


def third_kernel(window_ref, data_ref, *args):
    stars_ref, rest_ref, first_ref, grad_ref, image_ref, q_ref, row_ref, old_ref = args[:8]
    new_ref, x_ref, direction_ref, kept_ref, scalar_ref, work_ref = args[8:]
    inverse, length, gamma0, delta0 = kept(old_ref)[:4]
    gamma1, square1, cross1 = get_scalars(rest_ref)
    beta = gamma1 / gamma0
    first, grad = first_ref[...], grad_ref[...]
    direction = grad + beta * first
    q = row_ref[...] + beta * q_ref[...]
    delta1 = square1 + 2.0 * beta * cross1 + beta * beta * delta0
    image = read_sums(stars_ref, rest_ref) + beta * image_ref[...]
    step = gamma1 / delta1
    x_ref[...] = (gamma0 / delta0) * first + step * direction
    direction_ref[...] = direction
    grad = grad - step * image
    new_ref[...] = grad
    keep([inverse, length, gamma1, delta1], kept_ref)
    apply(window_ref[0], new_ref, data_ref, inverse, work_ref)
    row = work_ref[...]
    lane = iota((1, LO), 1)
    scalar_ref[...] = (
        jnp.where(lane == 0, square(grad), 0.0)
        + jnp.where(lane == 1, total(row * row), 0.0)
        + jnp.where(lane == 2, total(row * q), 0.0)
    )


def last_kernel(window_ref, sums_ref, grad_ref, x_ref, direction_ref, old_ref, *args):
    star_ref, att_ref, cal_ref, out_ref = args
    inverse, length, gamma1, delta1 = kept(old_ref)[:4]
    sums = jnp.sum(sums_ref[...], axis=0, keepdims=True)
    gamma2, square2, cross2 = (sums[:, i : i + 1] for i in range(3))
    beta = gamma2 / gamma1
    delta2 = square2 + 2.0 * beta * cross2 + beta * beta * delta1
    direction = grad_ref[...] + beta * direction_ref[...]
    x = (x_ref[...] + (gamma2 / delta2) * direction) * (inverse * length)
    out_ref[...] = x
    for hi in range(32):
        for p in range(5):
            star_ref[p : p + 1, LO * hi : LO * hi + LO] = x[32 * p + hi : 32 * p + hi + 1]
    knots, _ = with_heads(out_ref, window_ref[0], member_of(window_ref[0]))
    for a in range(3):
        for hi in range(8):
            att_ref[a : a + 1, LO * hi : LO * hi + LO] = knots[a][hi : hi + 1]
    cal_ref[...] = x[N_S : N_S + N_C]


def call(kernel, smem, vmem, outs, scratch=(), space=pltpu.VMEM, mebibytes=40):
    return pl.pallas_call(
        kernel,
        out_shape=[jax.ShapeDtypeStruct(shape, F32) for shape in outs],
        in_specs=[pl.BlockSpec(memory_space=pltpu.SMEM)] * len(smem)
        + [pl.BlockSpec(memory_space=space)] * len(vmem),
        out_specs=[pl.BlockSpec(memory_space=pltpu.VMEM)] * len(outs),
        scratch_shapes=list(scratch),
        compiler_params=pltpu.CompilerParams(vmem_limit_bytes=mebibytes * 1024 * 1024),
    )(*smem, *vmem)


def swap(value, axis, bits):
    count = lax.axis_size(axis)
    return lax.ppermute(value, axis, [(i, i ^ bits) for i in range(count)])


def add_swapped(value, axis, bits):
    arrived = [swap(value, axis, one) for one in bits]
    if len(bits) == 1:
        return value + arrived[0]
    return (value + arrived[0]) + (arrived[1] + arrived[2])


def over_star(rest):
    for bits in ((1,), (8, 24, 16), (2, 6, 4)):
        rest = add_swapped(rest, "star", bits)
    return rest


def share(data):
    near, wrap = swap(data, TM, 2), swap(data, TM, 6)
    half = ROWS // 2
    far = [swap(wrap[..., :half], TM, 2), swap(near[..., half:], TM, 6)]
    return jnp.concatenate([data, near, jnp.concatenate(far, axis=2), wrap], axis=0)


def reduce(wide, knots):
    wide = add_swapped(wide, TM, REST)
    return wide[:N_S], over_star(jnp.concatenate([wide[N_S:], knots], axis=0))


def shards(star_coef, att_coef, cal_coef, observed, star_index, knot_index, cal_index, valid_blocks):
    window = lax.axis_index(TM).astype(jnp.int32).reshape(1)
    arrays = (
        star_coef,
        att_coef,
        cal_coef.reshape(1, ROWS),
        observed.reshape(1, ROWS),
        star_index.reshape(1, ROWS),
        knot_index.reshape(1, ROWS),
        cal_index.reshape(1, ROWS),
    )
    wide_shape, vec_shape, small = (N_Z, LO), (N_ALL, LO), (8, LO)
    row_shape = (GROUP, ROWS)
    sums = (wide_shape, (N_K * GROUP, LO))
    scratch = [pltpu.VMEM((2 * N_S, LO), F32), pltpu.VMEM((2 * N_C, LO), F32)]
    (data,) = call(
        start_kernel,
        (valid_blocks,),
        arrays,
        ((1, PACKED, ROWS),),
        [pltpu.VMEM(item.shape, item.dtype) for item in arrays] + [pltpu.SemaphoreType.DMA((7,))],
        pltpu.HBM,
        60,
    )
    data = share(data)
    wide, knots = call(gather_kernel, (window,), (data,), sums, scratch)
    arrived = reduce(wide, knots)
    wide, knots, grad0, row0, scalars = call(
        first_kernel,
        (window,),
        (data,) + arrived,
        sums + (vec_shape, row_shape, small),
        scratch,
    )
    arrived = reduce(wide, knots)
    wide, knots, grad1, image0, row1, scalars = call(
        second_kernel,
        (window,),
        (data,) + arrived + (grad0, row0, scalars),
        sums + (vec_shape, vec_shape, row_shape, small),
        scratch,
    )
    arrived = reduce(wide, knots)
    grad2, x, direction, scalars, partial = call(
        third_kernel,
        (window,),
        (data,) + arrived + (grad0, grad1, image0, row0, row1, scalars),
        (vec_shape, vec_shape, vec_shape, small, (1, LO)),
        [pltpu.VMEM(row_shape, F32)],
    )
    axes = ("tm_low", "star")
    count = lax.axis_size(axes)
    everyone = lax.all_to_all(jnp.broadcast_to(partial[None], (count, 1, LO)), axes, 0, 0)
    stars, attitude, cals = call(
        last_kernel,
        (window,),
        (everyone.reshape(count, LO), grad2, x, direction, scalars),
        ((5, 4096), (3, 1024), (N_C, LO)),
        [pltpu.VMEM(vec_shape, F32)],
    )
    return stars, attitude, cals.reshape(-1)


def solution(mesh):
    split_mesh = Mesh(mesh.devices.reshape(4, 2, 32), TM + ("star",))
    by_row = P(TM + ("star",))
    return jax.shard_map(
        shards,
        mesh=split_mesh,
        in_specs=(P(None, TM + ("star",)),) * 2 + (by_row,) * 5 + (P(TM, "star"),),
        out_specs=(P(None, "star"), P(None, TM), P()),
        check_vma=False,
    )
```

```python
import jax
import jax.numpy as jnp
from jax import lax
from jax.experimental import pallas as pl
from jax.experimental.pallas import tpu as pltpu
from jax.sharding import Mesh
from jax.sharding import PartitionSpec as P

ROWS = 2048
LO = 128
MASKS = (0, 2, 4, 6)
REST = (1,)
GROUP = len(MASKS)
BITS = 0
for _mask in MASKS:
    BITS |= _mask
N_S, N_C, N_B, N_K = 160, 16, 8, 24
N_Z = N_S + N_C + N_B
N_ALL = N_Z + N_K * GROUP
STAR, ATT, CAL, INDEX, RIGHT, PACKED = 0, 5, 17, 18, 21, 24
PARTS = ((STAR, 5, 32), (ATT, 12, 8), (CAL, 1, 16))
SCALAR_LANE = 64
TM = ("tm_high", "tm_low")
F32, BF16 = jnp.float32, jnp.bfloat16


def iota(shape, axis):
    return lax.broadcasted_iota(jnp.int32, shape, axis)


def member_of(window):
    return (window >> 1) & (GROUP - 1)


def window_of(window, member):
    return (window & ~BITS) | (member << 1)


def split(value):
    first = value.astype(BF16)
    return first, (value - first.astype(F32)).astype(BF16)


def total(value):
    return jnp.sum(jnp.sum(value, axis=1, keepdims=True), axis=0, keepdims=True)


def one_hot(index, count):
    return jnp.where(iota((count, index.shape[1]), 0) == index, 1.0, 0.0)


def left_shift(knots, following, j):
    if j == 0:
        return knots
    rolled = pltpu.roll(knots, LO - j, 1)
    upper = pltpu.roll(rolled, 7, 0)
    ahead = pltpu.roll(jnp.broadcast_to(following, (8, LO)), LO - j, 1)
    upper = jnp.where(iota((8, LO), 0) == 7, ahead, upper)
    return jnp.where(iota((8, LO), 1) < LO - j, rolled, upper)


def head_rows(bounds, window):
    row = jnp.sum(jnp.where(iota((8, LO), 0) == window, bounds, 0.0), axis=0, keepdims=True)
    lane = iota((1, LO), 1)
    return [
        jnp.where(lane < 3, row if a == 0 else pltpu.roll(row, LO - 8 * a, 1), 0.0) for a in range(3)
    ]


def with_heads(vec_ref, window, member):
    bounds = vec_ref[N_S + N_C : N_Z]
    own, following = head_rows(bounds, window), head_rows(bounds, window + 1)
    knots = []
    for a in range(3):
        part = vec_ref[pl.ds(pl.multiple_of(N_Z + N_K * member + 8 * a, 8), 8)]
        knots.append(part + jnp.where(iota((8, LO), 0) == 0, jnp.broadcast_to(own[a], (8, LO)), 0.0))
    return knots, following


def shifted_knots(vec_ref, window, member):
    knots, following = with_heads(vec_ref, window, member)
    return jnp.concatenate(
        [left_shift(knots[a], following[a], j) for j in range(4) for a in range(3)], axis=0
    )


def hots_of(data_ref, slot, kinds):
    places = iota((LO, ROWS), 0).astype(F32).astype(BF16)
    hots = []
    for kind in kinds:
        index = data_ref[slot, INDEX + kind : INDEX + kind + 1].astype(jnp.int32)
        low = (index & (LO - 1)).astype(F32).astype(BF16)
        low = jnp.where(places == low, jnp.ones((), BF16), jnp.zeros((), BF16))
        hots.append((PARTS[kind], low, one_hot(index >> 7, PARTS[kind][2])))
    return hots


def forward(data_ref, slot, hots, tables):
    result = None
    for ((base, coefs, count), low, high), table in zip(hots, tables):
        taken = jnp.dot(table, jnp.concatenate([low, low], axis=0), preferred_element_type=F32)
        mixed = None
        for p in range(coefs):
            term = data_ref[slot, base + p : base + p + 1] * taken[p * count : (p + 1) * count]
            mixed = term if mixed is None else mixed + term
        mixed = mixed * high
        for part in range(0, count, 8):
            piece = mixed[part : part + 8]
            result = piece if result is None else result + piece
    return jnp.sum(result, axis=0, keepdims=True)


def adjoint(data_ref, slot, hots, row):
    sums = []
    for (base, coefs, count), low, high in hots:
        pieces = split(data_ref[slot, base : base + coefs] * row)
        left = jnp.concatenate(
            [
                (high * piece[p : p + 1].astype(F32)).astype(BF16)
                for piece in pieces
                for p in range(coefs)
            ],
            axis=0,
        )
        sums.append(lax.dot_general(left, low, (((1,), (1,)), ((), ())), preferred_element_type=F32))
    return sums


def fold(sums):
    return sums[: sums.shape[0] // 2] + sums[sums.shape[0] // 2 :]


def knot_sums(spread, window):
    rows, lanes = iota((8, LO), 0), iota((8, LO), 1)
    knots, heads, tails = [], 0.0, 0.0
    for a in range(3):
        own, over = spread[8 * a : 8 * a + 8], jnp.zeros((8, LO), F32)
        for j in range(1, 4):
            rolled = pltpu.roll(spread[24 * j + 8 * a : 24 * j + 8 * a + 8], j, 1)
            wrapped = pltpu.roll(rolled, 1, 0)
            own = own + jnp.where(lanes >= j, rolled, jnp.where(rows > 0, wrapped, 0.0))
            over = over + jnp.where(lanes < j, wrapped, 0.0)
        is_head = jnp.logical_and(rows == 0, lanes < 3)
        knots.append(jnp.where(is_head, 0.0, own))
        head, tail = jnp.where(is_head, own, 0.0), jnp.where(rows == 0, over, 0.0)
        if a > 0:
            head, tail = pltpu.roll(head, 8 * a, 1), pltpu.roll(tail, 8 * a, 1)
        heads, tails = heads + head, tails + tail
    head = jnp.broadcast_to(heads[:1], (8, LO))
    tail = jnp.broadcast_to(tails[:1], (8, LO))
    bounds = jnp.where(rows == window, head, 0.0) + jnp.where(rows == window + 1, tail, 0.0)
    return jnp.concatenate(knots, axis=0), bounds


def set_scalars(rest_ref, scalars):
    rows, lanes = iota((8, LO), 0), iota((8, LO), 1)
    block = rest_ref[N_C : N_C + N_B]
    for i, scalar in enumerate(scalars):
        here = jnp.logical_and(rows == i, lanes == SCALAR_LANE)
        block = jnp.where(here, jnp.broadcast_to(scalar, (8, LO)), block)
    rest_ref[N_C : N_C + N_B] = block


def get_scalars(rest_ref):
    bounds = rest_ref[N_C : N_C + N_B]
    rows, lanes = iota((8, LO), 0), iota((8, LO), 1)
    return [
        total(jnp.where(jnp.logical_and(rows == i, lanes == SCALAR_LANE), bounds, 0.0)) for i in range(3)
    ]


def read_sums(stars_ref, rest_ref):
    bounds = jnp.where(iota((8, LO), 1) < SCALAR_LANE, rest_ref[N_C : N_C + N_B], 0.0)
    return jnp.concatenate([stars_ref[...], rest_ref[:N_C], bounds, rest_ref[N_C + N_B :]], axis=0)


def square(vec):
    part = vec * vec
    return (
        total(part[:N_S]) * (GROUP / 8)
        + total(part[N_S:N_Z]) * (GROUP / 256)
        + total(part[N_Z:]) * (1 / 32)
    )


def keep(scalars, ref):
    rows = iota((8, LO), 0)
    block = jnp.zeros((8, LO), F32)
    for i, scalar in enumerate(scalars):
        block = jnp.where(rows == i, jnp.broadcast_to(scalar, (8, LO)), block)
    ref[...] = block


def kept(ref):
    return [ref[i : i + 1, 0:1] for i in range(8)]


def start_kernel(blocks_ref, *args):
    sources, data_ref, scratch = args[:7], args[7], args[8:]
    held, semaphore = scratch[:7], scratch[7]
    copies = [
        pltpu.make_async_copy(source, target, semaphore.at[i])
        for i, (source, target) in enumerate(zip(sources, held))
    ]
    for copy in copies:
        copy.start()
    for copy in copies:
        copy.wait()
    live = jnp.where(iota((1, ROWS), 1) < 128 * blocks_ref[0, 0], 1.0, 0.0)
    data_ref[0, STAR : STAR + 5] = held[0][...] * live
    data_ref[0, ATT : ATT + 12] = held[1][...] * live
    data_ref[0, CAL : CAL + 1] = held[2][...] * live
    for which in range(3):
        data_ref[0, INDEX + which : INDEX + which + 1] = held[4 + which][...].astype(F32)
    data_ref[0, RIGHT : RIGHT + 1] = held[3][...] * live
    data_ref[0, RIGHT + 1 :] = jnp.zeros((PACKED - RIGHT - 1, ROWS), F32)


def clear(refs):
    for ref in refs:
        ref[...] = jnp.zeros(ref.shape, F32)


def add_sums(data_ref, slot, hots, row, window, member, rest_ref, cal_ref):
    spread, cals = adjoint(data_ref, slot, hots, row)
    cal_ref[...] += cals
    knots, bounds = knot_sums(fold(spread), window_of(window, member))
    at = N_C + N_B + N_K * member
    rest_ref[at : at + N_K] = knots
    rest_ref[N_C : N_C + N_B] += bounds


def table_of(rows):
    return jnp.concatenate(split(rows), axis=1)


def knot_table(vec_ref, window, member):
    return table_of(shifted_knots(vec_ref, window_of(window, member), member))


def right_kernel(window_ref, data_ref, rest_ref, cal_ref):
    window = window_ref[0]
    clear((rest_ref, cal_ref))
    norm, size = 0.0, 0.0
    for member in range(GROUP):
        slot = member_of(window) ^ member
        row = data_ref[slot, RIGHT : RIGHT + 1]
        coefs = data_ref[slot, :INDEX]
        norm += total(row * row)
        size += total(jnp.sum(coefs * coefs, axis=0, keepdims=True))
        hots = hots_of(data_ref, slot, (1, 2))
        add_sums(data_ref, slot, hots, row, window, member, rest_ref, cal_ref)
    rest_ref[:N_C] = fold(cal_ref[...])
    set_scalars(rest_ref, [norm, size])


def right_stars_kernel(window_ref, data_ref, out_ref, star_ref):
    clear((star_ref,))
    for member in range(GROUP):
        slot = member_of(window_ref[0]) ^ member
        row = data_ref[slot, RIGHT : RIGHT + 1]
        star_ref[...] += adjoint(data_ref, slot, hots_of(data_ref, slot, (0,)), row)[0]
    out_ref[...] = fold(star_ref[...])


def stars_kernel(window_ref, data_ref, row_ref, kept_ref, out_ref, star_ref):
    clear((star_ref,))
    inverse = kept(kept_ref)[0]
    for member in range(GROUP):
        slot = member_of(window_ref[0]) ^ member
        row = row_ref[member : member + 1] * inverse
        star_ref[...] += adjoint(data_ref, slot, hots_of(data_ref, slot, (0,)), row)[0]
    out_ref[...] = fold(star_ref[...])


def taken_kernel(window_ref, data_ref, stars_ref, kept_ref, out_ref):
    inverse = kept(kept_ref)[0]
    table = table_of(stars_ref[...])
    for member in range(GROUP):
        slot = member_of(window_ref[0]) ^ member
        hots = hots_of(data_ref, slot, (0,))
        out_ref[member : member + 1] = forward(data_ref, slot, hots, (table,)) * inverse


def first_kernel(window_ref, data_ref, stars_ref, rest_in_ref, *args):
    rest_ref, grad_ref, row_ref, kept_ref, cal_ref = args
    window = window_ref[0]
    norm, size, _ = get_scalars(rest_in_ref)
    inverse, length = lax.rsqrt(size), jnp.sqrt(norm)
    grad = read_sums(stars_ref, rest_in_ref) * inverse / length
    grad_ref[...] = grad
    keep([inverse, length], kept_ref)
    clear((rest_ref, cal_ref))
    star_table, cal_table = table_of(grad[:N_S]), table_of(grad[N_S : N_S + N_C])
    for member in range(GROUP):
        slot = member_of(window) ^ member
        hots = hots_of(data_ref, slot, (0, 1, 2))
        tables = (star_table, knot_table(grad_ref, window, member), cal_table)
        row = forward(data_ref, slot, hots, tables) * inverse
        row_ref[member : member + 1] = row
        add_sums(data_ref, slot, hots[1:], row * inverse, window, member, rest_ref, cal_ref)
    rest_ref[:N_C] = fold(cal_ref[...])
    row = row_ref[...]
    set_scalars(rest_ref, [square(grad), total(row * row)])


def second_kernel(window_ref, data_ref, *args):
    stars_ref, rest_in_ref, taken_ref, grad_ref, q_ref, old_ref = args[:6]
    rest_ref, new_ref, image_ref, mapped_ref, row_ref, kept_ref, cal_ref = args[6:]
    window = window_ref[0]
    inverse, length = kept(old_ref)[:2]
    gamma, delta, _ = get_scalars(rest_in_ref)
    step = gamma / delta
    image = read_sums(stars_ref, rest_in_ref)
    image_ref[...] = image
    grad = grad_ref[...] - step * image
    new_ref[...] = grad
    keep([inverse, length, gamma, delta], kept_ref)
    clear((rest_ref, cal_ref))
    cal_table = table_of(image[N_S : N_S + N_C])
    for member in range(GROUP):
        slot = member_of(window) ^ member
        own = slice(member, member + 1)
        hots = hots_of(data_ref, slot, (1, 2))
        tables = (knot_table(image_ref, window, member), cal_table)
        mapped = taken_ref[own] + forward(data_ref, slot, hots, tables) * inverse
        mapped_ref[own] = mapped
        row = q_ref[own] - step * mapped
        row_ref[own] = row
        add_sums(data_ref, slot, hots, row * inverse, window, member, rest_ref, cal_ref)
    rest_ref[:N_C] = fold(cal_ref[...])
    row = row_ref[...]
    set_scalars(rest_ref, [square(grad), total(row * row), total(row * q_ref[...])])


def third_kernel(window_ref, data_ref, *args):
    stars_ref, rest_in_ref, taken_ref, first_ref, grad_ref, image_ref, mapped_ref = args[:7]
    q_ref, row_ref, old_ref = args[7:10]
    new_ref, x_ref, direction_ref, kept_ref, scalar_ref, work_ref, raw_ref = args[10:]
    window = window_ref[0]
    inverse, length, gamma0, delta0 = kept(old_ref)[:4]
    gamma1, square1, cross1 = get_scalars(rest_in_ref)
    beta = gamma1 / gamma0
    first, grad = first_ref[...], grad_ref[...]
    direction = grad + beta * first
    q = row_ref[...] + beta * q_ref[...]
    delta1 = square1 + 2.0 * beta * cross1 + beta * beta * delta0
    raw = read_sums(stars_ref, rest_in_ref)
    raw_ref[...] = raw
    step = gamma1 / delta1
    x_ref[...] = (gamma0 / delta0) * first + step * direction
    direction_ref[...] = direction
    grad = grad - step * (raw + beta * image_ref[...])
    new_ref[...] = grad
    keep([inverse, length, gamma1, delta1], kept_ref)
    cal_table = table_of(raw[N_S : N_S + N_C])
    for member in range(GROUP):
        slot = member_of(window) ^ member
        own = slice(member, member + 1)
        hots = hots_of(data_ref, slot, (1, 2))
        tables = (knot_table(raw_ref, window, member), cal_table)
        mapped = taken_ref[own] + forward(data_ref, slot, hots, tables) * inverse
        work_ref[own] = row_ref[own] - step * (mapped + beta * mapped_ref[own])
    row = work_ref[...]
    lane = iota((1, LO), 1)
    scalar_ref[...] = (
        jnp.where(lane == 0, square(grad), 0.0)
        + jnp.where(lane == 1, total(row * row), 0.0)
        + jnp.where(lane == 2, total(row * q), 0.0)
    )


def last_kernel(window_ref, sums_ref, grad_ref, x_ref, direction_ref, old_ref, *args):
    star_ref, att_ref, cal_ref, out_ref = args
    inverse, length, gamma1, delta1 = kept(old_ref)[:4]
    sums = jnp.sum(sums_ref[...], axis=0, keepdims=True)
    gamma2, square2, cross2 = (sums[:, i : i + 1] for i in range(3))
    beta = gamma2 / gamma1
    delta2 = square2 + 2.0 * beta * cross2 + beta * beta * delta1
    direction = grad_ref[...] + beta * direction_ref[...]
    x = (x_ref[...] + (gamma2 / delta2) * direction) * (inverse * length)
    out_ref[...] = x
    for hi in range(32):
        for p in range(5):
            star_ref[p : p + 1, LO * hi : LO * hi + LO] = x[32 * p + hi : 32 * p + hi + 1]
    knots, _ = with_heads(out_ref, window_ref[0], member_of(window_ref[0]))
    for a in range(3):
        for hi in range(8):
            att_ref[a : a + 1, LO * hi : LO * hi + LO] = knots[a][hi : hi + 1]
    cal_ref[...] = x[N_S : N_S + N_C]


def call(kernel, smem, vmem, outs, scratch=(), space=pltpu.VMEM, mebibytes=40):
    return pl.pallas_call(
        kernel,
        out_shape=[jax.ShapeDtypeStruct(shape, F32) for shape in outs],
        in_specs=[pl.BlockSpec(memory_space=pltpu.SMEM)] * len(smem)
        + [pl.BlockSpec(memory_space=space)] * len(vmem),
        out_specs=[pl.BlockSpec(memory_space=pltpu.VMEM)] * len(outs),
        scratch_shapes=list(scratch),
        cost_estimate=pl.CostEstimate(flops=1500000000, bytes_accessed=1000000, transcendentals=0),
        compiler_params=pltpu.CompilerParams(vmem_limit_bytes=mebibytes * 1024 * 1024),
    )(*smem, *vmem)


def swap(value, axis, bits):
    count = lax.axis_size(axis)
    return lax.ppermute(value, axis, [(i, i ^ bits) for i in range(count)])


def add_swapped(value, axis, bits):
    arrived = [swap(value, axis, one) for one in bits]
    if len(bits) == 1:
        return value + arrived[0]
    return (value + arrived[0]) + (arrived[1] + arrived[2])


def share(data):
    near, wrap = swap(data, TM, 2), swap(data, TM, 6)
    half = ROWS // 2
    far = [swap(wrap[..., :half], TM, 2), swap(near[..., half:], TM, 6)]
    return jnp.concatenate([data, near, jnp.concatenate(far, axis=2), wrap], axis=0)


def reduce(rest, add_stars, take_stars=None):
    bounded = add_swapped(rest[: N_C + N_B], TM, REST)
    bounded, stars = lax.optimization_barrier((bounded, add_stars()))
    stars = add_swapped(stars, TM, REST)
    rest = jnp.concatenate([bounded, rest[N_C + N_B :]], axis=0)
    rest = add_swapped(add_swapped(rest, "star", (1,)), "star", (8, 24, 16))
    rest, stars = lax.optimization_barrier((rest, stars))
    taken = () if take_stars is None else (take_stars(stars),)
    return (stars, add_swapped(rest, "star", (2, 6, 4))) + taken


def shards(star_coef, att_coef, cal_coef, observed, star_index, knot_index, cal_index, valid_blocks):
    window = lax.axis_index(TM).astype(jnp.int32).reshape(1)
    arrays = (
        star_coef,
        att_coef,
        cal_coef.reshape(1, ROWS),
        observed.reshape(1, ROWS),
        star_index.reshape(1, ROWS),
        knot_index.reshape(1, ROWS),
        cal_index.reshape(1, ROWS),
    )
    vec_shape, small, row_shape = (N_ALL, LO), (8, LO), (GROUP, ROWS)
    rest_shape = (N_ALL - N_S, LO)
    star_scratch, cal_scratch = [pltpu.VMEM((2 * N_S, LO), F32)], [pltpu.VMEM((2 * N_C, LO), F32)]
    (data,) = call(
        start_kernel,
        (valid_blocks,),
        arrays,
        ((1, PACKED, ROWS),),
        [pltpu.VMEM(item.shape, item.dtype) for item in arrays] + [pltpu.SemaphoreType.DMA((7,))],
        pltpu.HBM,
        60,
    )
    data = share(data)

    def star_sums(row, kept_scalars):
        return call(stars_kernel, (window,), (data, row, kept_scalars), ((N_S, LO),), star_scratch)[0]

    def taken(stars, kept_scalars):
        return call(taken_kernel, (window,), (data, stars, kept_scalars), (row_shape,))[0]

    (rest,) = call(right_kernel, (window,), (data,), (rest_shape,), cal_scratch)
    arrived = reduce(
        rest, lambda: call(right_stars_kernel, (window,), (data,), ((N_S, LO),), star_scratch)[0]
    )
    rest, grad0, row0, scalars0 = call(
        first_kernel, (window,), (data,) + arrived, (rest_shape, vec_shape, row_shape, small), cal_scratch
    )
    arrived = reduce(rest, lambda: star_sums(row0, scalars0), lambda stars: taken(stars, scalars0))
    rest, grad1, image0, mapped0, row1, scalars1 = call(
        second_kernel,
        (window,),
        (data,) + arrived + (grad0, row0, scalars0),
        (rest_shape, vec_shape, vec_shape, row_shape, row_shape, small),
        cal_scratch,
    )
    arrived = reduce(rest, lambda: star_sums(row1, scalars1), lambda stars: taken(stars, scalars1))
    grad2, x, direction, scalars, partial = call(
        third_kernel,
        (window,),
        (data,) + arrived + (grad0, grad1, image0, mapped0, row0, row1, scalars1),
        (vec_shape, vec_shape, vec_shape, small, (1, LO)),
        [pltpu.VMEM(row_shape, F32), pltpu.VMEM(vec_shape, F32)],
    )
    axes = ("tm_low", "star")
    count = lax.axis_size(axes)
    everyone = lax.all_to_all(jnp.broadcast_to(partial[None], (count, 1, LO)), axes, 0, 0)
    stars, attitude, cals = call(
        last_kernel,
        (window,),
        (everyone.reshape(count, LO), grad2, x, direction, scalars),
        ((5, 4096), (3, 1024), (N_C, LO)),
        [pltpu.VMEM(vec_shape, F32)],
    )
    return stars, attitude, cals.reshape(-1)


def solution(mesh):
    split_mesh = Mesh(mesh.devices.reshape(4, 2, 32), TM + ("star",))
    by_row = P(TM + ("star",))
    return jax.shard_map(
        shards,
        mesh=split_mesh,
        in_specs=(P(None, TM + ("star",)),) * 2 + (by_row,) * 5 + (P(TM, "star"),),
        out_specs=(P(None, "star"), P(None, TM), P()),
        check_vma=False,
    )
```

```python
import jax
import jax.numpy as jnp
from jax import lax
from jax.experimental import pallas as pl
from jax.experimental.pallas import tpu as pltpu
from jax.sharding import Mesh
from jax.sharding import PartitionSpec as P

ROWS = 2048
HALF = ROWS // 2
LO = 128
MASKS = (0, 2, 4, 6)
REST = (1,)
GROUP = len(MASKS)
BITS = 0
for _mask in MASKS:
    BITS |= _mask
N_S, N_C, N_B, N_K = 160, 16, 8, 24
N_Z = N_S + N_C + N_B
N_ALL = N_Z + N_K * GROUP
STAR, ATT, CAL, INDEX, RIGHT, PACKED = 0, 5, 17, 18, 21, 24
PARTS = ((STAR, 5, 32), (ATT, 12, 8), (CAL, 1, 16))
SCALAR_LANE = 64
TM = ("tm_high", "tm_low")
F32, BF16 = jnp.float32, jnp.bfloat16


def iota(shape, axis):
    return lax.broadcasted_iota(jnp.int32, shape, axis)


def member_of(window):
    return (window >> 1) & (GROUP - 1)


def window_of(window, member):
    return (window & ~BITS) | (member << 1)


def split(value):
    first = value.astype(BF16)
    return first, (value - first.astype(F32)).astype(BF16)


def total(value):
    return jnp.sum(jnp.sum(value, axis=1, keepdims=True), axis=0, keepdims=True)


def one_hot(index, count):
    return jnp.where(iota((count, index.shape[1]), 0) == index, 1.0, 0.0)


def left_shift(knots, following, j):
    if j == 0:
        return knots
    rolled = pltpu.roll(knots, LO - j, 1)
    upper = pltpu.roll(rolled, 7, 0)
    ahead = pltpu.roll(jnp.broadcast_to(following, (8, LO)), LO - j, 1)
    upper = jnp.where(iota((8, LO), 0) == 7, ahead, upper)
    return jnp.where(iota((8, LO), 1) < LO - j, rolled, upper)


def head_rows(bounds, window):
    row = jnp.sum(jnp.where(iota((8, LO), 0) == window, bounds, 0.0), axis=0, keepdims=True)
    lane = iota((1, LO), 1)
    return [
        jnp.where(lane < 3, row if a == 0 else pltpu.roll(row, LO - 8 * a, 1), 0.0) for a in range(3)
    ]


def with_heads(vec_ref, window, member):
    bounds = vec_ref[N_S + N_C : N_Z]
    own, following = head_rows(bounds, window), head_rows(bounds, window + 1)
    knots = []
    for a in range(3):
        part = vec_ref[pl.ds(pl.multiple_of(N_Z + N_K * member + 8 * a, 8), 8)]
        knots.append(part + jnp.where(iota((8, LO), 0) == 0, jnp.broadcast_to(own[a], (8, LO)), 0.0))
    return knots, following


def shifted_knots(vec_ref, window, member):
    knots, following = with_heads(vec_ref, window, member)
    return jnp.concatenate(
        [left_shift(knots[a], following[a], j) for j in range(4) for a in range(3)], axis=0
    )


def hots_of(data_ref, slot, kinds):
    places = iota((LO, data_ref.shape[2]), 0).astype(F32).astype(BF16)
    hots = []
    for kind in kinds:
        index = data_ref[slot, INDEX + kind : INDEX + kind + 1].astype(jnp.int32)
        low = (index & (LO - 1)).astype(F32).astype(BF16)
        low = jnp.where(places == low, jnp.ones((), BF16), jnp.zeros((), BF16))
        hots.append((PARTS[kind], low, one_hot(index >> 7, PARTS[kind][2])))
    return hots


def forward(data_ref, slot, hots, tables):
    result = None
    for ((base, coefs, count), low, high), table in zip(hots, tables):
        taken = jnp.dot(table, jnp.concatenate([low, low], axis=0), preferred_element_type=F32)
        mixed = None
        for p in range(coefs):
            term = data_ref[slot, base + p : base + p + 1] * taken[p * count : (p + 1) * count]
            mixed = term if mixed is None else mixed + term
        mixed = mixed * high
        for part in range(0, count, 8):
            piece = mixed[part : part + 8]
            result = piece if result is None else result + piece
    return jnp.sum(result, axis=0, keepdims=True)


def adjoint(data_ref, slot, hots, row):
    sums = []
    for (base, coefs, count), low, high in hots:
        pieces = split(data_ref[slot, base : base + coefs] * row)
        left = jnp.concatenate(
            [
                (high * piece[p : p + 1].astype(F32)).astype(BF16)
                for piece in pieces
                for p in range(coefs)
            ],
            axis=0,
        )
        sums.append(lax.dot_general(left, low, (((1,), (1,)), ((), ())), preferred_element_type=F32))
    return sums


def fold(sums):
    return sums[: sums.shape[0] // 2] + sums[sums.shape[0] // 2 :]


def knot_sums(spread, window):
    rows, lanes = iota((8, LO), 0), iota((8, LO), 1)
    knots, heads, tails = [], 0.0, 0.0
    for a in range(3):
        own, over = spread[8 * a : 8 * a + 8], jnp.zeros((8, LO), F32)
        for j in range(1, 4):
            rolled = pltpu.roll(spread[24 * j + 8 * a : 24 * j + 8 * a + 8], j, 1)
            wrapped = pltpu.roll(rolled, 1, 0)
            own = own + jnp.where(lanes >= j, rolled, jnp.where(rows > 0, wrapped, 0.0))
            over = over + jnp.where(lanes < j, wrapped, 0.0)
        is_head = jnp.logical_and(rows == 0, lanes < 3)
        knots.append(jnp.where(is_head, 0.0, own))
        head, tail = jnp.where(is_head, own, 0.0), jnp.where(rows == 0, over, 0.0)
        if a > 0:
            head, tail = pltpu.roll(head, 8 * a, 1), pltpu.roll(tail, 8 * a, 1)
        heads, tails = heads + head, tails + tail
    head = jnp.broadcast_to(heads[:1], (8, LO))
    tail = jnp.broadcast_to(tails[:1], (8, LO))
    bounds = jnp.where(rows == window, head, 0.0) + jnp.where(rows == window + 1, tail, 0.0)
    return jnp.concatenate(knots, axis=0), bounds


def set_scalars(rest_ref, scalars):
    rows, lanes = iota((8, LO), 0), iota((8, LO), 1)
    block = rest_ref[N_C : N_C + N_B]
    for i, scalar in enumerate(scalars):
        here = jnp.logical_and(rows == i, lanes == SCALAR_LANE)
        block = jnp.where(here, jnp.broadcast_to(scalar, (8, LO)), block)
    rest_ref[N_C : N_C + N_B] = block


def get_scalars(rest_ref):
    bounds = rest_ref[N_C : N_C + N_B]
    rows, lanes = iota((8, LO), 0), iota((8, LO), 1)
    return [
        total(jnp.where(jnp.logical_and(rows == i, lanes == SCALAR_LANE), bounds, 0.0)) for i in range(3)
    ]


def read_sums(stars_ref, rest_ref):
    bounds = jnp.where(iota((8, LO), 1) < SCALAR_LANE, rest_ref[N_C : N_C + N_B], 0.0)
    return jnp.concatenate([stars_ref[...], rest_ref[:N_C], bounds, rest_ref[N_C + N_B :]], axis=0)


def square(vec):
    part = vec * vec
    return (
        total(part[:N_S]) * (GROUP / 8)
        + total(part[N_S:N_Z]) * (GROUP / 256)
        + total(part[N_Z:]) * (1 / 32)
    )


def keep(scalars, ref):
    rows = iota((8, LO), 0)
    block = jnp.zeros((8, LO), F32)
    for i, scalar in enumerate(scalars):
        block = jnp.where(rows == i, jnp.broadcast_to(scalar, (8, LO)), block)
    ref[...] = block


def kept(ref):
    return [ref[i : i + 1, 0:1] for i in range(8)]


def start_kernel(blocks_ref, *args):
    sources, halves, scratch = args[:7], args[7:9], args[9:]
    held, semaphore = scratch[:7], scratch[7]
    copies = [
        pltpu.make_async_copy(source, target, semaphore.at[i])
        for i, (source, target) in enumerate(zip(sources, held))
    ]
    for copy in copies:
        copy.start()
    for copy in copies:
        copy.wait()
    live = jnp.where(iota((1, ROWS), 1) < 128 * blocks_ref[0, 0], 1.0, 0.0)
    for half, data_ref in enumerate(halves):
        columns = slice(HALF * half, HALF * half + HALF)
        here = live[:, columns]
        data_ref[0, STAR : STAR + 5] = held[0][:, columns] * here
        data_ref[0, ATT : ATT + 12] = held[1][:, columns] * here
        data_ref[0, CAL : CAL + 1] = held[2][:, columns] * here
        for which in range(3):
            data_ref[0, INDEX + which : INDEX + which + 1] = held[4 + which][:, columns].astype(F32)
        data_ref[0, RIGHT : RIGHT + 1] = held[3][:, columns] * here
        data_ref[0, RIGHT + 1 :] = jnp.zeros((PACKED - RIGHT - 1, HALF), F32)


def clear(refs):
    for ref in refs:
        ref[...] = jnp.zeros(ref.shape, F32)


def add_sums(data_ref, slot, hots, row, window, member, rest_ref, cal_ref):
    spread, cals = adjoint(data_ref, slot, hots, row)
    cal_ref[...] += cals
    knots, bounds = knot_sums(fold(spread), window_of(window, member))
    at = N_C + N_B + N_K * member
    rest_ref[at : at + N_K] = knots
    rest_ref[N_C : N_C + N_B] += bounds


def table_of(rows):
    return jnp.concatenate(split(rows), axis=1)


def knot_table(vec_ref, window, member):
    return table_of(shifted_knots(vec_ref, window_of(window, member), member))


def right_kernel(window_ref, data_ref, rest_ref, cal_ref):
    window = window_ref[0]
    clear((rest_ref, cal_ref))
    norm, size = 0.0, 0.0
    for member in range(GROUP):
        slot = member_of(window) ^ member
        row = data_ref[slot, RIGHT : RIGHT + 1]
        coefs = data_ref[slot, :INDEX]
        norm += total(row * row)
        size += total(jnp.sum(coefs * coefs, axis=0, keepdims=True))
        hots = hots_of(data_ref, slot, (1, 2))
        add_sums(data_ref, slot, hots, row, window, member, rest_ref, cal_ref)
    rest_ref[:N_C] = fold(cal_ref[...])
    set_scalars(rest_ref, [norm, size])


def right_stars_kernel(window_ref, data_ref, out_ref, star_ref):
    clear((star_ref,))
    for member in range(GROUP):
        slot = member_of(window_ref[0]) ^ member
        row = data_ref[slot, RIGHT : RIGHT + 1]
        star_ref[...] += adjoint(data_ref, slot, hots_of(data_ref, slot, (0,)), row)[0]
    out_ref[...] = fold(star_ref[...])


def stars_kernel(window_ref, data_ref, row_ref, kept_ref, out_ref, star_ref):
    clear((star_ref,))
    inverse = kept(kept_ref)[0]
    for member in range(GROUP):
        slot = member_of(window_ref[0]) ^ member
        row = row_ref[member : member + 1] * inverse
        star_ref[...] += adjoint(data_ref, slot, hots_of(data_ref, slot, (0,)), row)[0]
    out_ref[...] = fold(star_ref[...])


def taken_kernel(window_ref, data_ref, stars_ref, kept_ref, out_ref):
    inverse = kept(kept_ref)[0]
    table = table_of(stars_ref[...])
    for member in range(GROUP):
        slot = member_of(window_ref[0]) ^ member
        hots = hots_of(data_ref, slot, (0,))
        out_ref[member : member + 1] = forward(data_ref, slot, hots, (table,)) * inverse


def first_taken_kernel(window_ref, data_ref, stars_ref, out_ref, biggest_ref):
    stars = stars_ref[...]
    biggest = jnp.max(jnp.max(jnp.abs(stars), axis=1, keepdims=True), axis=0, keepdims=True)
    biggest = jnp.where(biggest > 0.0, biggest, 1.0)
    biggest_ref[...] = jnp.broadcast_to(biggest, (8, LO))
    table = table_of(stars / biggest)
    for member in range(GROUP):
        slot = member_of(window_ref[0]) ^ member
        hots = hots_of(data_ref, slot, (0,))
        out_ref[member : member + 1] = forward(data_ref, slot, hots, (table,))


def first_kernel(window_ref, data_ref, stars_ref, rest_in_ref, taken_ref, biggest_ref, *args):
    rest_ref, grad_ref, row_ref, kept_ref, cal_ref = args
    window = window_ref[0]
    norm, size, _ = get_scalars(rest_in_ref)
    inverse, length = lax.rsqrt(size), jnp.sqrt(norm)
    grad = read_sums(stars_ref, rest_in_ref) * inverse / length
    grad_ref[...] = grad
    keep([inverse, length], kept_ref)
    clear((rest_ref, cal_ref))
    cal_table = table_of(grad[N_S : N_S + N_C])
    share = biggest_ref[0:1, 0:1] * inverse / length
    for member in range(GROUP):
        slot = member_of(window) ^ member
        own = slice(member, member + 1)
        hots = hots_of(data_ref, slot, (1, 2))
        tables = (knot_table(grad_ref, window, member), cal_table)
        row = (taken_ref[own] * share + forward(data_ref, slot, hots, tables)) * inverse
        row_ref[own] = row
        add_sums(data_ref, slot, hots, row * inverse, window, member, rest_ref, cal_ref)
    rest_ref[:N_C] = fold(cal_ref[...])
    row = row_ref[...]
    set_scalars(rest_ref, [square(grad), total(row * row)])


def second_kernel(window_ref, data_ref, *args):
    stars_ref, rest_in_ref, taken_ref, grad_ref, q_ref, old_ref = args[:6]
    rest_ref, new_ref, image_ref, mapped_ref, row_ref, kept_ref, cal_ref = args[6:]
    window = window_ref[0]
    inverse, length = kept(old_ref)[:2]
    gamma, delta, _ = get_scalars(rest_in_ref)
    step = gamma / delta
    image = read_sums(stars_ref, rest_in_ref)
    image_ref[...] = image
    grad = grad_ref[...] - step * image
    new_ref[...] = grad
    keep([inverse, length, gamma, delta], kept_ref)
    clear((rest_ref, cal_ref))
    cal_table = table_of(image[N_S : N_S + N_C])
    for member in range(GROUP):
        slot = member_of(window) ^ member
        own = slice(member, member + 1)
        hots = hots_of(data_ref, slot, (1, 2))
        tables = (knot_table(image_ref, window, member), cal_table)
        mapped = taken_ref[own] + forward(data_ref, slot, hots, tables) * inverse
        mapped_ref[own] = mapped
        row = q_ref[own] - step * mapped
        row_ref[own] = row
        add_sums(data_ref, slot, hots, row * inverse, window, member, rest_ref, cal_ref)
    rest_ref[:N_C] = fold(cal_ref[...])
    row = row_ref[...]
    set_scalars(rest_ref, [square(grad), total(row * row), total(row * q_ref[...])])


def third_kernel(window_ref, data_ref, *args):
    stars_ref, rest_in_ref, taken_ref, first_ref, grad_ref, image_ref, mapped_ref = args[:7]
    q_ref, row_ref, old_ref = args[7:10]
    new_ref, x_ref, direction_ref, kept_ref, scalar_ref, work_ref, raw_ref = args[10:]
    window = window_ref[0]
    inverse, length, gamma0, delta0 = kept(old_ref)[:4]
    gamma1, square1, cross1 = get_scalars(rest_in_ref)
    beta = gamma1 / gamma0
    first, grad = first_ref[...], grad_ref[...]
    direction = grad + beta * first
    q = row_ref[...] + beta * q_ref[...]
    delta1 = square1 + 2.0 * beta * cross1 + beta * beta * delta0
    raw = read_sums(stars_ref, rest_in_ref)
    raw_ref[...] = raw
    step = gamma1 / delta1
    x_ref[...] = (gamma0 / delta0) * first + step * direction
    direction_ref[...] = direction
    grad = grad - step * (raw + beta * image_ref[...])
    new_ref[...] = grad
    keep([inverse, length, gamma1, delta1], kept_ref)
    cal_table = table_of(raw[N_S : N_S + N_C])
    for member in range(GROUP):
        slot = member_of(window) ^ member
        own = slice(member, member + 1)
        hots = hots_of(data_ref, slot, (1, 2))
        tables = (knot_table(raw_ref, window, member), cal_table)
        mapped = taken_ref[own] + forward(data_ref, slot, hots, tables) * inverse
        work_ref[own] = row_ref[own] - step * (mapped + beta * mapped_ref[own])
    row = work_ref[...]
    lane = iota((1, LO), 1)
    scalar_ref[...] = (
        jnp.where(lane == 0, square(grad), 0.0)
        + jnp.where(lane == 1, total(row * row), 0.0)
        + jnp.where(lane == 2, total(row * q), 0.0)
    )


def last_kernel(window_ref, sums_ref, grad_ref, x_ref, direction_ref, old_ref, *args):
    star_ref, att_ref, cal_ref, out_ref = args
    inverse, length, gamma1, delta1 = kept(old_ref)[:4]
    sums = jnp.sum(sums_ref[...], axis=0, keepdims=True)
    gamma2, square2, cross2 = (sums[:, i : i + 1] for i in range(3))
    beta = gamma2 / gamma1
    delta2 = square2 + 2.0 * beta * cross2 + beta * beta * delta1
    direction = grad_ref[...] + beta * direction_ref[...]
    x = (x_ref[...] + (gamma2 / delta2) * direction) * (inverse * length)
    out_ref[...] = x
    for hi in range(32):
        for p in range(5):
            star_ref[p : p + 1, LO * hi : LO * hi + LO] = x[32 * p + hi : 32 * p + hi + 1]
    knots, _ = with_heads(out_ref, window_ref[0], member_of(window_ref[0]))
    for a in range(3):
        for hi in range(8):
            att_ref[a : a + 1, LO * hi : LO * hi + LO] = knots[a][hi : hi + 1]
    cal_ref[...] = x[N_S : N_S + N_C]


def call(kernel, smem, vmem, outs, scratch=(), space=pltpu.VMEM, mebibytes=40):
    return pl.pallas_call(
        kernel,
        out_shape=[jax.ShapeDtypeStruct(shape, F32) for shape in outs],
        in_specs=[pl.BlockSpec(memory_space=pltpu.SMEM)] * len(smem)
        + [pl.BlockSpec(memory_space=space)] * len(vmem),
        out_specs=[pl.BlockSpec(memory_space=pltpu.VMEM)] * len(outs),
        scratch_shapes=list(scratch),
        cost_estimate=pl.CostEstimate(flops=1500000000, bytes_accessed=1000000, transcendentals=0),
        compiler_params=pltpu.CompilerParams(vmem_limit_bytes=mebibytes * 1024 * 1024),
    )(*smem, *vmem)


def swap(value, axis, bits):
    count = lax.axis_size(axis)
    return lax.ppermute(value, axis, [(i, i ^ bits) for i in range(count)])


def add_swapped(value, axis, bits):
    arrived = [swap(value, axis, one) for one in bits]
    if len(bits) == 1:
        return value + arrived[0]
    return (value + arrived[0]) + (arrived[1] + arrived[2])


def share(left, right):
    near_right, wrap_left = swap(right, TM, 2), swap(left, TM, 6)
    near_left, wrap_right = swap(left, TM, 2), swap(right, TM, 6)
    far_left, far_right = swap(wrap_left, TM, 2), swap(near_right, TM, 6)
    return (
        (left, right),
        (near_left, near_right),
        (far_left, far_right),
        (wrap_left, wrap_right),
    )


def reduce(rest, add_stars, take_stars):
    bounded = add_swapped(rest[: N_C + N_B], TM, REST)
    bounded, stars = lax.optimization_barrier((bounded, add_stars()))
    stars = add_swapped(stars, TM, REST)
    rest = jnp.concatenate([bounded, rest[N_C + N_B :]], axis=0)
    rest = add_swapped(add_swapped(rest, "star", (1,)), "star", (8, 24, 16))
    rest, stars = lax.optimization_barrier((rest, stars))
    taken = take_stars(stars)
    return [stars, add_swapped(rest, "star", (2, 6, 4)), *taken]


def shards(star_coef, att_coef, cal_coef, observed, star_index, knot_index, cal_index, valid_blocks):
    window = lax.axis_index(TM).astype(jnp.int32).reshape(1)
    arrays = (
        star_coef,
        att_coef,
        cal_coef.reshape(1, ROWS),
        observed.reshape(1, ROWS),
        star_index.reshape(1, ROWS),
        knot_index.reshape(1, ROWS),
        cal_index.reshape(1, ROWS),
    )
    vec_shape, small, row_shape = (N_ALL, LO), (8, LO), (GROUP, ROWS)
    rest_shape = (N_ALL - N_S, LO)
    star_scratch, cal_scratch = [pltpu.VMEM((2 * N_S, LO), F32)], [pltpu.VMEM((2 * N_C, LO), F32)]
    halves = call(
        start_kernel,
        (valid_blocks,),
        arrays,
        ((1, PACKED, HALF),) * 2,
        [pltpu.VMEM(item.shape, item.dtype) for item in arrays] + [pltpu.SemaphoreType.DMA((7,))],
        pltpu.HBM,
        60,
    )
    shared = share(*halves)
    data = jnp.concatenate([jnp.concatenate(pair, axis=2) for pair in shared], axis=0)

    def star_sums(row, kept_scalars):
        return call(stars_kernel, (window,), (data, row, kept_scalars), ((N_S, LO),), star_scratch)[0]

    def taken(stars, kept_scalars):
        return call(taken_kernel, (window,), (data, stars, kept_scalars), (row_shape,))

    (rest,) = call(right_kernel, (window,), (data,), (rest_shape,), cal_scratch)
    arrived = reduce(
        rest,
        lambda: call(right_stars_kernel, (window,), (data,), ((N_S, LO),), star_scratch)[0],
        lambda stars: call(first_taken_kernel, (window,), (data, stars), (row_shape, small)),
    )
    rest, grad0, row0, scalars0 = call(
        first_kernel, (window,), [data] + arrived, (rest_shape, vec_shape, row_shape, small), cal_scratch
    )
    arrived = reduce(rest, lambda: star_sums(row0, scalars0), lambda stars: taken(stars, scalars0))
    rest, grad1, image0, mapped0, row1, scalars1 = call(
        second_kernel,
        (window,),
        [data] + arrived + [grad0, row0, scalars0],
        (rest_shape, vec_shape, vec_shape, row_shape, row_shape, small),
        cal_scratch,
    )
    arrived = reduce(rest, lambda: star_sums(row1, scalars1), lambda stars: taken(stars, scalars1))
    grad2, x, direction, scalars, partial = call(
        third_kernel,
        (window,),
        [data] + arrived + [grad0, grad1, image0, mapped0, row0, row1, scalars1],
        (vec_shape, vec_shape, vec_shape, small, (1, LO)),
        [pltpu.VMEM(row_shape, F32), pltpu.VMEM(vec_shape, F32)],
    )
    axes = ("tm_low", "star")
    count = lax.axis_size(axes)
    everyone = lax.all_to_all(jnp.broadcast_to(partial[None], (count, 1, LO)), axes, 0, 0)
    stars, attitude, cals = call(
        last_kernel,
        (window,),
        (everyone.reshape(count, LO), grad2, x, direction, scalars),
        ((5, 4096), (3, 1024), (N_C, LO)),
        [pltpu.VMEM(vec_shape, F32)],
    )
    return stars, attitude, cals.reshape(-1)


def solution(mesh):
    split_mesh = Mesh(mesh.devices.reshape(4, 2, 32), TM + ("star",))
    by_row = P(TM + ("star",))
    return jax.shard_map(
        shards,
        mesh=split_mesh,
        in_specs=(P(None, TM + ("star",)),) * 2 + (by_row,) * 5 + (P(TM, "star"),),
        out_specs=(P(None, "star"), P(None, TM), P()),
        check_vma=False,
    )
```

```python
import jax
import jax.numpy as jnp
from jax import lax
from jax.experimental import pallas as pl
from jax.experimental.pallas import tpu as pltpu
from jax.sharding import Mesh
from jax.sharding import PartitionSpec as P

ROWS = 2048
HALF = ROWS // 2
LO = 128
MASKS = (0, 2, 4, 6)
REST = (1,)
GROUP = len(MASKS)
BITS = 0
for _mask in MASKS:
    BITS |= _mask
N_S, N_C, N_B, N_K = 160, 16, 8, 24
N_Z = N_S + N_C + N_B
N_ALL = N_Z + N_K * GROUP
STAR, ATT, CAL, INDEX, RIGHT, PACKED = 0, 5, 17, 18, 21, 24
PARTS = ((STAR, 5, 32), (ATT, 12, 8), (CAL, 1, 16))
SCALAR_LANE = 64
TM = ("tm_high", "tm_low")
F32, BF16 = jnp.float32, jnp.bfloat16


def iota(shape, axis):
    return lax.broadcasted_iota(jnp.int32, shape, axis)


def member_of(window):
    return (window >> 1) & (GROUP - 1)


def window_of(window, member):
    return (window & ~BITS) | (member << 1)


def split(value):
    first = value.astype(BF16)
    return first, (value - first.astype(F32)).astype(BF16)


def total(value):
    return jnp.sum(jnp.sum(value, axis=0, keepdims=True), axis=1, keepdims=True)


def one_hot(index, count):
    return jnp.where(iota((count, index.shape[1]), 0) == index, 1.0, 0.0)


def left_shift(knots, following, j):
    if j == 0:
        return knots
    rolled = pltpu.roll(knots, LO - j, 1)
    upper = pltpu.roll(rolled, 7, 0)
    ahead = pltpu.roll(jnp.broadcast_to(following, (8, LO)), LO - j, 1)
    upper = jnp.where(iota((8, LO), 0) == 7, ahead, upper)
    return jnp.where(iota((8, LO), 1) < LO - j, rolled, upper)


def head_rows(bounds, window):
    row = jnp.sum(jnp.where(iota((8, LO), 0) == window, bounds, 0.0), axis=0, keepdims=True)
    lane = iota((1, LO), 1)
    return [
        jnp.where(lane < 3, row if a == 0 else pltpu.roll(row, LO - 8 * a, 1), 0.0) for a in range(3)
    ]


def with_heads(vec_ref, window, member):
    bounds = vec_ref[N_S + N_C : N_Z]
    own, following = head_rows(bounds, window), head_rows(bounds, window + 1)
    knots = []
    for a in range(3):
        part = vec_ref[pl.ds(pl.multiple_of(N_Z + N_K * member + 8 * a, 8), 8)]
        knots.append(part + jnp.where(iota((8, LO), 0) == 0, jnp.broadcast_to(own[a], (8, LO)), 0.0))
    return knots, following


def shifted_knots(vec_ref, window, member):
    knots, following = with_heads(vec_ref, window, member)
    return jnp.concatenate(
        [left_shift(knots[a], following[a], j) for j in range(4) for a in range(3)], axis=0
    )


def hots_of(data_ref, slot, kinds):
    places = iota((LO, data_ref.shape[2]), 0).astype(F32).astype(BF16)
    hots = []
    for kind in kinds:
        index = data_ref[slot, INDEX + kind : INDEX + kind + 1].astype(jnp.int32)
        low = (index & (LO - 1)).astype(F32).astype(BF16)
        low = jnp.where(places == low, jnp.ones((), BF16), jnp.zeros((), BF16))
        hots.append((PARTS[kind], low, one_hot(index >> 7, PARTS[kind][2])))
    return hots


def forward(data_ref, slot, hots, tables):
    result = None
    for ((base, coefs, count), low, high), table in zip(hots, tables):
        taken = jnp.dot(table, jnp.concatenate([low, low], axis=0), preferred_element_type=F32)
        mixed = None
        for p in range(coefs):
            term = data_ref[slot, base + p : base + p + 1] * taken[p * count : (p + 1) * count]
            mixed = term if mixed is None else mixed + term
        mixed = mixed * high
        for part in range(0, count, 8):
            piece = mixed[part : part + 8]
            result = piece if result is None else result + piece
    return jnp.sum(result, axis=0, keepdims=True)


def adjoint(data_ref, slot, hots, row):
    sums = []
    for (base, coefs, count), low, high in hots:
        pieces = split(data_ref[slot, base : base + coefs] * row)
        left = jnp.concatenate(
            [
                (high * piece[p : p + 1].astype(F32)).astype(BF16)
                for piece in pieces
                for p in range(coefs)
            ],
            axis=0,
        )
        sums.append(lax.dot_general(left, low, (((1,), (1,)), ((), ())), preferred_element_type=F32))
    return sums


def fold(sums):
    return sums[: sums.shape[0] // 2] + sums[sums.shape[0] // 2 :]


def knot_sums(spread, window):
    rows, lanes = iota((8, LO), 0), iota((8, LO), 1)
    knots, heads, tails = [], 0.0, 0.0
    for a in range(3):
        own, over = spread[8 * a : 8 * a + 8], jnp.zeros((8, LO), F32)
        for j in range(1, 4):
            rolled = pltpu.roll(spread[24 * j + 8 * a : 24 * j + 8 * a + 8], j, 1)
            wrapped = pltpu.roll(rolled, 1, 0)
            own = own + jnp.where(lanes >= j, rolled, jnp.where(rows > 0, wrapped, 0.0))
            over = over + jnp.where(lanes < j, wrapped, 0.0)
        is_head = jnp.logical_and(rows == 0, lanes < 3)
        knots.append(jnp.where(is_head, 0.0, own))
        head, tail = jnp.where(is_head, own, 0.0), jnp.where(rows == 0, over, 0.0)
        if a > 0:
            head, tail = pltpu.roll(head, 8 * a, 1), pltpu.roll(tail, 8 * a, 1)
        heads, tails = heads + head, tails + tail
    head = jnp.broadcast_to(heads[:1], (8, LO))
    tail = jnp.broadcast_to(tails[:1], (8, LO))
    bounds = jnp.where(rows == window, head, 0.0) + jnp.where(rows == window + 1, tail, 0.0)
    return jnp.concatenate(knots, axis=0), bounds


def set_scalars(rest_ref, scalars):
    rows, lanes = iota((8, LO), 0), iota((8, LO), 1)
    block = rest_ref[N_C : N_C + N_B]
    for i, scalar in enumerate(scalars):
        here = jnp.logical_and(rows == i, lanes == SCALAR_LANE)
        block = jnp.where(here, jnp.broadcast_to(scalar, (8, LO)), block)
    rest_ref[N_C : N_C + N_B] = block


def get_scalars(rest_ref):
    lanes = slice(SCALAR_LANE, SCALAR_LANE + 1)
    return [rest_ref[N_C + i : N_C + i + 1, lanes] for i in range(3)]


def read_sums(stars_ref, rest_ref):
    bounds = jnp.where(iota((8, LO), 1) < SCALAR_LANE, rest_ref[N_C : N_C + N_B], 0.0)
    return jnp.concatenate([stars_ref[...], rest_ref[:N_C], bounds, rest_ref[N_C + N_B :]], axis=0)


def square(vec):
    part = vec * vec
    return (
        total(part[:N_S]) * (GROUP / 8)
        + total(part[N_S:N_Z]) * (GROUP / 256)
        + total(part[N_Z:]) * (1 / 32)
    )


def keep(scalars, ref):
    rows = iota((8, LO), 0)
    block = jnp.zeros((8, LO), F32)
    for i, scalar in enumerate(scalars):
        block = jnp.where(rows == i, jnp.broadcast_to(scalar, (8, LO)), block)
    ref[...] = block


def kept(ref):
    return [ref[i : i + 1, 0:1] for i in range(8)]


def start_kernel(blocks_ref, *args):
    sources, halves, scratch = args[:7], args[7:9], args[9:]
    held, semaphore = scratch[:7], scratch[7]
    copies = [
        pltpu.make_async_copy(source, target, semaphore.at[i])
        for i, (source, target) in enumerate(zip(sources, held))
    ]
    for copy in copies:
        copy.start()
    for copy in copies:
        copy.wait()
    live = jnp.where(iota((1, ROWS), 1) < 128 * blocks_ref[0, 0], 1.0, 0.0)
    for half, data_ref in enumerate(halves):
        columns = slice(HALF * half, HALF * half + HALF)
        here = live[:, columns]
        data_ref[0, STAR : STAR + 5] = held[0][:, columns] * here
        data_ref[0, ATT : ATT + 12] = held[1][:, columns] * here
        data_ref[0, CAL : CAL + 1] = held[2][:, columns] * here
        for which in range(3):
            data_ref[0, INDEX + which : INDEX + which + 1] = held[4 + which][:, columns].astype(F32)
        data_ref[0, RIGHT : RIGHT + 1] = held[3][:, columns] * here
        data_ref[0, RIGHT + 1 :] = jnp.zeros((PACKED - RIGHT - 1, HALF), F32)


def clear(refs):
    for ref in refs:
        ref[...] = jnp.zeros(ref.shape, F32)


def add_sums(data_ref, slot, hots, row, window, member, rest_ref, cal_ref):
    spread, cals = adjoint(data_ref, slot, hots, row)
    cal_ref[...] += cals
    knots, bounds = knot_sums(fold(spread), window_of(window, member))
    at = N_C + N_B + N_K * member
    rest_ref[at : at + N_K] = knots
    rest_ref[N_C : N_C + N_B] += bounds


def table_of(rows):
    return jnp.concatenate(split(rows), axis=1)


def knot_table(vec_ref, window, member):
    return table_of(shifted_knots(vec_ref, window_of(window, member), member))


def right_kernel(window_ref, data_ref, rest_ref, cal_ref):
    window = window_ref[0]
    clear((rest_ref, cal_ref))
    norm, size = 0.0, 0.0
    for member in range(GROUP):
        slot = member_of(window) ^ member
        row = data_ref[slot, RIGHT : RIGHT + 1]
        coefs = data_ref[slot, :INDEX]
        norm += total(row * row)
        size += total(jnp.sum(coefs * coefs, axis=0, keepdims=True))
        hots = hots_of(data_ref, slot, (1, 2))
        add_sums(data_ref, slot, hots, row, window, member, rest_ref, cal_ref)
    rest_ref[:N_C] = fold(cal_ref[...])
    set_scalars(rest_ref, [norm, size])


def right_stars_kernel(window_ref, data_ref, out_ref, star_ref):
    clear((star_ref,))
    for member in range(GROUP):
        slot = member_of(window_ref[0]) ^ member
        row = data_ref[slot, RIGHT : RIGHT + 1]
        star_ref[...] += adjoint(data_ref, slot, hots_of(data_ref, slot, (0,)), row)[0]
    out_ref[...] = fold(star_ref[...])


def stars_kernel(window_ref, data_ref, row_ref, kept_ref, out_ref, star_ref):
    clear((star_ref,))
    inverse = kept(kept_ref)[0]
    for member in range(GROUP):
        slot = member_of(window_ref[0]) ^ member
        row = row_ref[member : member + 1] * inverse
        star_ref[...] += adjoint(data_ref, slot, hots_of(data_ref, slot, (0,)), row)[0]
    out_ref[...] = fold(star_ref[...])


def taken_kernel(window_ref, data_ref, stars_ref, kept_ref, out_ref):
    inverse = kept(kept_ref)[0]
    table = table_of(stars_ref[...])
    for member in range(GROUP):
        slot = member_of(window_ref[0]) ^ member
        hots = hots_of(data_ref, slot, (0,))
        out_ref[member : member + 1] = forward(data_ref, slot, hots, (table,)) * inverse


def first_taken_kernel(window_ref, data_ref, stars_ref, out_ref, biggest_ref):
    stars = stars_ref[...]
    biggest = jnp.max(jnp.max(jnp.abs(stars), axis=1, keepdims=True), axis=0, keepdims=True)
    biggest = jnp.where(biggest > 0.0, biggest, 1.0)
    biggest_ref[...] = jnp.broadcast_to(biggest, (8, LO))
    table = table_of(stars / biggest)
    for member in range(GROUP):
        slot = member_of(window_ref[0]) ^ member
        hots = hots_of(data_ref, slot, (0,))
        out_ref[member : member + 1] = forward(data_ref, slot, hots, (table,))


def first_kernel(window_ref, data_ref, stars_ref, rest_in_ref, taken_ref, biggest_ref, *args):
    rest_ref, grad_ref, row_ref, kept_ref, cal_ref = args
    window = window_ref[0]
    norm, size, _ = get_scalars(rest_in_ref)
    inverse, length = lax.rsqrt(size), jnp.sqrt(norm)
    grad = read_sums(stars_ref, rest_in_ref) * inverse / length
    grad_ref[...] = grad
    keep([inverse, length], kept_ref)
    clear((rest_ref, cal_ref))
    cal_table = table_of(grad[N_S : N_S + N_C])
    share = biggest_ref[0:1, 0:1] * inverse / length
    for member in range(GROUP):
        slot = member_of(window) ^ member
        own = slice(member, member + 1)
        hots = hots_of(data_ref, slot, (1, 2))
        tables = (knot_table(grad_ref, window, member), cal_table)
        row = (taken_ref[own] * share + forward(data_ref, slot, hots, tables)) * inverse
        row_ref[own] = row
        add_sums(data_ref, slot, hots, row * inverse, window, member, rest_ref, cal_ref)
    rest_ref[:N_C] = fold(cal_ref[...])
    row = row_ref[...]
    set_scalars(rest_ref, [square(grad), total(row * row)])


def second_kernel(window_ref, data_ref, *args):
    stars_ref, rest_in_ref, taken_ref, grad_ref, q_ref, old_ref = args[:6]
    rest_ref, new_ref, image_ref, mapped_ref, row_ref, kept_ref, cal_ref = args[6:]
    window = window_ref[0]
    inverse, length = kept(old_ref)[:2]
    gamma, delta, _ = get_scalars(rest_in_ref)
    step = gamma / delta
    image = read_sums(stars_ref, rest_in_ref)
    image_ref[...] = image
    grad = grad_ref[...] - step * image
    new_ref[...] = grad
    keep([inverse, length, gamma, delta], kept_ref)
    clear((rest_ref, cal_ref))
    cal_table = table_of(image[N_S : N_S + N_C])
    for member in range(GROUP):
        slot = member_of(window) ^ member
        own = slice(member, member + 1)
        hots = hots_of(data_ref, slot, (1, 2))
        tables = (knot_table(image_ref, window, member), cal_table)
        mapped = taken_ref[own] + forward(data_ref, slot, hots, tables) * inverse
        mapped_ref[own] = mapped
        row = q_ref[own] - step * mapped
        row_ref[own] = row
        add_sums(data_ref, slot, hots, row * inverse, window, member, rest_ref, cal_ref)
    rest_ref[:N_C] = fold(cal_ref[...])
    row = row_ref[...]
    set_scalars(rest_ref, [square(grad), total(row * row), total(row * q_ref[...])])


def third_kernel(window_ref, data_ref, *args):
    stars_ref, rest_in_ref, taken_ref, first_ref, grad_ref, image_ref, mapped_ref = args[:7]
    q_ref, row_ref, old_ref = args[7:10]
    new_ref, x_ref, direction_ref, kept_ref, scalar_ref, work_ref, raw_ref = args[10:]
    window = window_ref[0]
    inverse, length, gamma0, delta0 = kept(old_ref)[:4]
    gamma1, square1, cross1 = get_scalars(rest_in_ref)
    beta = gamma1 / gamma0
    first, grad = first_ref[...], grad_ref[...]
    direction = grad + beta * first
    q = row_ref[...] + beta * q_ref[...]
    delta1 = square1 + 2.0 * beta * cross1 + beta * beta * delta0
    raw = read_sums(stars_ref, rest_in_ref)
    raw_ref[...] = raw
    step = gamma1 / delta1
    x_ref[...] = (gamma0 / delta0) * first + step * direction
    direction_ref[...] = direction
    grad = grad - step * (raw + beta * image_ref[...])
    new_ref[...] = grad
    keep([inverse, length, gamma1, delta1], kept_ref)
    cal_table = table_of(raw[N_S : N_S + N_C])
    for member in range(GROUP):
        slot = member_of(window) ^ member
        own = slice(member, member + 1)
        hots = hots_of(data_ref, slot, (1, 2))
        tables = (knot_table(raw_ref, window, member), cal_table)
        mapped = taken_ref[own] + forward(data_ref, slot, hots, tables) * inverse
        work_ref[own] = row_ref[own] - step * (mapped + beta * mapped_ref[own])
    row = work_ref[...]
    lane = iota((1, LO), 1)
    scalar_ref[...] = (
        jnp.where(lane == 0, square(grad), 0.0)
        + jnp.where(lane == 1, total(row * row), 0.0)
        + jnp.where(lane == 2, total(row * q), 0.0)
    )


def last_kernel(window_ref, sums_ref, grad_ref, x_ref, direction_ref, old_ref, *args):
    star_ref, att_ref, cal_ref, out_ref = args
    inverse, length, gamma1, delta1 = kept(old_ref)[:4]
    sums = jnp.sum(sums_ref[...], axis=0, keepdims=True)
    gamma2, square2, cross2 = (sums[:, i : i + 1] for i in range(3))
    beta = gamma2 / gamma1
    delta2 = square2 + 2.0 * beta * cross2 + beta * beta * delta1
    direction = grad_ref[...] + beta * direction_ref[...]
    x = (x_ref[...] + (gamma2 / delta2) * direction) * (inverse * length)
    out_ref[...] = x
    for hi in range(32):
        for p in range(5):
            star_ref[p : p + 1, LO * hi : LO * hi + LO] = x[32 * p + hi : 32 * p + hi + 1]
    knots, _ = with_heads(out_ref, window_ref[0], member_of(window_ref[0]))
    for a in range(3):
        for hi in range(8):
            att_ref[a : a + 1, LO * hi : LO * hi + LO] = knots[a][hi : hi + 1]
    cal_ref[...] = x[N_S : N_S + N_C]


def call(kernel, smem, vmem, outs, scratch=(), space=pltpu.VMEM, mebibytes=40):
    return pl.pallas_call(
        kernel,
        out_shape=[jax.ShapeDtypeStruct(shape, F32) for shape in outs],
        in_specs=[pl.BlockSpec(memory_space=pltpu.SMEM)] * len(smem)
        + [pl.BlockSpec(memory_space=space)] * len(vmem),
        out_specs=[pl.BlockSpec(memory_space=pltpu.VMEM)] * len(outs),
        scratch_shapes=list(scratch),
        cost_estimate=pl.CostEstimate(flops=1500000000, bytes_accessed=1000000, transcendentals=0),
        compiler_params=pltpu.CompilerParams(vmem_limit_bytes=mebibytes * 1024 * 1024),
    )(*smem, *vmem)


def swap(value, axis, bits):
    count = lax.axis_size(axis)
    return lax.ppermute(value, axis, [(i, i ^ bits) for i in range(count)])


def add_swapped(value, axis, bits):
    arrived = [swap(value, axis, one) for one in bits]
    if len(bits) == 1:
        return value + arrived[0]
    return (value + arrived[0]) + (arrived[1] + arrived[2])


def share(left, right):
    near_right, wrap_left = swap(right, TM, 2), swap(left, TM, 6)
    near_left, wrap_right = swap(left, TM, 2), swap(right, TM, 6)
    far_left, far_right = swap(wrap_left, TM, 2), swap(near_right, TM, 6)
    return (
        (left, right),
        (near_left, near_right),
        (far_left, far_right),
        (wrap_left, wrap_right),
    )


def reduce(rest, add_stars, take_stars):
    bounded = add_swapped(rest[: N_C + N_B], TM, REST)
    bounded, stars = lax.optimization_barrier((bounded, add_stars()))
    stars = add_swapped(stars, TM, REST)
    rest = jnp.concatenate([bounded, rest[N_C + N_B :]], axis=0)
    rest = add_swapped(add_swapped(rest, "star", (1,)), "star", (8, 24, 16))
    rest, stars = lax.optimization_barrier((rest, stars))
    taken = take_stars(stars)
    return [stars, add_swapped(rest, "star", (2, 6, 4)), *taken]


def shards(star_coef, att_coef, cal_coef, observed, star_index, knot_index, cal_index, valid_blocks):
    window = lax.axis_index(TM).astype(jnp.int32).reshape(1)
    arrays = (
        star_coef,
        att_coef,
        cal_coef.reshape(1, ROWS),
        observed.reshape(1, ROWS),
        star_index.reshape(1, ROWS),
        knot_index.reshape(1, ROWS),
        cal_index.reshape(1, ROWS),
    )
    vec_shape, small, row_shape = (N_ALL, LO), (8, LO), (GROUP, ROWS)
    rest_shape = (N_ALL - N_S, LO)
    star_scratch, cal_scratch = [pltpu.VMEM((2 * N_S, LO), F32)], [pltpu.VMEM((2 * N_C, LO), F32)]
    halves = call(
        start_kernel,
        (valid_blocks,),
        arrays,
        ((1, PACKED, HALF),) * 2,
        [pltpu.VMEM(item.shape, item.dtype) for item in arrays] + [pltpu.SemaphoreType.DMA((7,))],
        pltpu.HBM,
        60,
    )
    shared = share(*halves)
    data = jnp.concatenate([jnp.concatenate(pair, axis=2) for pair in shared], axis=0)

    def star_sums(row, kept_scalars):
        return call(stars_kernel, (window,), (data, row, kept_scalars), ((N_S, LO),), star_scratch)[0]

    def taken(stars, kept_scalars):
        return call(taken_kernel, (window,), (data, stars, kept_scalars), (row_shape,))

    (rest,) = call(right_kernel, (window,), (data,), (rest_shape,), cal_scratch)
    arrived = reduce(
        rest,
        lambda: call(right_stars_kernel, (window,), (data,), ((N_S, LO),), star_scratch)[0],
        lambda stars: call(first_taken_kernel, (window,), (data, stars), (row_shape, small)),
    )
    rest, grad0, row0, scalars0 = call(
        first_kernel, (window,), [data] + arrived, (rest_shape, vec_shape, row_shape, small), cal_scratch
    )
    arrived = reduce(rest, lambda: star_sums(row0, scalars0), lambda stars: taken(stars, scalars0))
    rest, grad1, image0, mapped0, row1, scalars1 = call(
        second_kernel,
        (window,),
        [data] + arrived + [grad0, row0, scalars0],
        (rest_shape, vec_shape, vec_shape, row_shape, row_shape, small),
        cal_scratch,
    )
    arrived = reduce(rest, lambda: star_sums(row1, scalars1), lambda stars: taken(stars, scalars1))
    grad2, x, direction, scalars, partial = call(
        third_kernel,
        (window,),
        [data] + arrived + [grad0, grad1, image0, mapped0, row0, row1, scalars1],
        (vec_shape, vec_shape, vec_shape, small, (1, LO)),
        [pltpu.VMEM(row_shape, F32), pltpu.VMEM(vec_shape, F32)],
    )
    axes = ("tm_low", "star")
    count = lax.axis_size(axes)
    everyone = lax.all_to_all(jnp.broadcast_to(partial[None], (count, 1, LO)), axes, 0, 0)
    stars, attitude, cals = call(
        last_kernel,
        (window,),
        (everyone.reshape(count, LO), grad2, x, direction, scalars),
        ((5, 4096), (3, 1024), (N_C, LO)),
        [pltpu.VMEM(vec_shape, F32)],
    )
    return stars, attitude, cals.reshape(-1)


def solution(mesh):
    split_mesh = Mesh(mesh.devices.reshape(4, 2, 32), TM + ("star",))
    by_row = P(TM + ("star",))
    return jax.shard_map(
        shards,
        mesh=split_mesh,
        in_specs=(P(None, TM + ("star",)),) * 2 + (by_row,) * 5 + (P(TM, "star"),),
        out_specs=(P(None, "star"), P(None, TM), P()),
        check_vma=False,
    )
```
